32 devices in a mesh: dp: 8 (over z, x), mp: 4 (over y, core).
Axes of the slice: x: 2, y: 2, z: 4, core: 2. Of those that a mesh axis runs over, the one named last changes fastest.
Arguments:
- tokens: bfloat16 [8192, 768], P('dp'), may hold values from -6 to 6
- cotangent: bfloat16 [8192, 768], P(('dp', 'mp')), may hold values from -6 to 6
- mix_coef: float32 [8192], P(('dp', 'mp')), may hold values from 0.25 to 0.75
- partner_dev: int32 [8192, 1], P(('dp', 'mp')), may hold values from 0 to 7; in each aligned block of 256 rows (0 to 255, 256 to 511, ...) at most 64 rows name the same one
- partner_row: int32 [8192], P(('dp', 'mp')), may hold values from 0 to 1023
- view_counts: int32 [8, 2], P('dp'), may hold values from 128 to 512
- w_qkv: bfloat16 [2, 768, 3, 768], P(None, None, None, 'mp'), may hold values from -0.21875 to 0.21875
- w_out: bfloat16 [2, 768, 768], P(None, 'mp'), may hold values from -1.75 to 1.75
- w_up: bfloat16 [2, 768, 3072], P(None, None, 'mp'), may hold values from -0.21875 to 0.21875
- w_down: bfloat16 [2, 3072, 768], P(None, 'mp'), may hold values from -0.109375 to 0.109375
- gain_attn: float32 [2, 768], replicated, may hold values from 0.1 to 1.9
- gain_mlp: float32 [2, 768], replicated, may hold values from 0.1 to 1.9
Outputs:
- layer_output: bfloat16 [8192, 768], P(('dp', 'mp'))
- grad_tokens: float32 [8192, 768], P(('dp', 'mp'))
- grad_qkv: float32 [2, 768, 3, 768], P(None, 'dp', None, 'mp')
- grad_out: float32 [2, 768, 768], P(None, 'mp', 'dp')
- grad_up: float32 [2, 768, 3072], P(None, 'dp', 'mp')
- grad_down: float32 [2, 3072, 768], P(None, 'mp', 'dp')
- grad_gain_attn: float32 [2, 768], P(None, 'dp')
- grad_gain_mlp: float32 [2, 768], P(None, 'dp')
The draws below stay inside these ranges and needn't reach their ends.
Inputs may be any that keep to these rules, and one draw needn't show every extreme that they name: `partner_dev`: in each aligned block of 256 rows no clip is named by more than 64 rows, a bound that some block reaches.
All inputs are finite; a program needn't handle non-finite values.
Results may differ from the reference program's by a relative error of at most 0.025.
The reference program's roundings to bfloat16 on the way count: a program that leaves them out, or rounds other values in their place, can miss the bound.
Values may be sent and summed in bfloat16 or wider, within the bound.
No kernel may reach another device: no remote copies, remote signals or barrier semaphores. Data moves between devices by JAX's collectives and lax.ppermute only.
A program may use at most 192 MiB of HBM per device.

```python
import math
import jax
import jax.numpy as jnp
import numpy as np
from jax import lax

D = 768
HEADS = 12
HD = 64
FF = 3072
VL = 512
ROWS_DEV = 1024
CLIPS = 8
TOKENS = 8192
QROWS = 256
CAP = 64
N_DP = 8


def place_ends(values, stream_key, low, largest):
    longest = values.shape.index(max(values.shape))
    spots = []
    for shift in (0, 1):
        where = [jax.random.randint(jax.random.fold_in(stream_key, axis), (), 0, length) for axis, length in enumerate(values.shape)]
        where[longest] = (where[longest] + shift) % values.shape[longest]
        spots.append(tuple(where))
    return values.at[spots[0]].set(low).at[spots[1]].set(largest)


def with_spikes(entries, key, source, target, blocks, factor):
    def block_of(position):
        return (jnp.arange(entries.shape[position]) // (entries.shape[position] // blocks)).reshape((-1,) + (1,) * (entries.ndim - 1 - position))

    one_side = jax.random.permutation(key, blocks)[block_of(target)]
    other_side = (block_of(target) + blocks // 2) % blocks
    return jnp.where((block_of(source) == one_side) | (block_of(source) == other_side), factor * entries, entries)


def steps_of(rng, shape, pieces, low, high):
    def one(axis_at, blocks):
        draws = jax.random.uniform(jax.random.fold_in(jax.random.fold_in(rng, 6), axis_at), (blocks,), jnp.float32, low / len(pieces), high / len(pieces))
        return jnp.repeat(jnp.exp(draws), shape[axis_at] // blocks).reshape((-1,) + (1,) * (len(shape) - axis_at - 1))

    loudness = one(*pieces[0])
    for cut in pieces[1:]:
        loudness = loudness * one(*cut)
    return loudness


def assign_block(key, own, number, rows, number_of, top, most, slope):
    order = jax.random.permutation(key, number_of)
    packed, usual = shares(number_of, rows * top, most, slope, True), shares(number_of, rows * top, most, slope, False)
    places = jnp.arange(number_of)

    def named(sizes, offset_by):
        used = int((sizes > 0).sum())
        fixed = max(1, used // 4)
        moved = fixed + (places - fixed + offset_by * (used - fixed)) % max(1, number_of - fixed)
        return jnp.zeros((number_of,), jnp.int32).at[order[jnp.where(places < fixed, places, moved)]].set(jnp.asarray(sizes, jnp.int32))

    sizes = jnp.where(number % 4 == 0, named(packed, number // 4), named(usual, number - number // 4 - 1))
    mixed = jax.random.permutation(jax.random.fold_in(own, 3), number_of)
    donor, receiver = mixed[0:number_of // 2 * 2:2], mixed[1:number_of // 2 * 2:2]
    margin = jnp.minimum(sizes[donor] - 1, most - sizes[receiver]) // 2
    margin = jnp.where((donor == order[0]) | (receiver == order[0]) | (sizes[receiver] == 0), 0, jnp.maximum(margin, 0))
    moved = jax.random.randint(jax.random.fold_in(own, 4), (number_of // 2,), 0, 1 << 20) % (margin + 1)
    sizes = sizes.at[donor].add(-moved).at[receiver].add(moved)
    items = jnp.searchsorted(jnp.cumsum(sizes), jnp.arange(rows * top), side="right").astype(jnp.int32)
    listing = items.reshape(top, rows).T
    listing = listing[jax.random.permutation(jax.random.fold_in(own, 1), rows)]
    offset_by = jax.random.randint(jax.random.fold_in(own, 2), (rows, 1), 0, top)
    return jnp.take_along_axis(listing, (jnp.arange(top)[None, :] + offset_by) % top, axis=1)


def shares(amount, total, most, lean, full):
    weights = [(1 << 20) // math.isqrt(standing ** lean) + 1 for standing in range(1, amount + 1)]
    largest = most if full else min(most, max(-(-total // amount), total * weights[0] // sum(weights)))
    least = 1 if total - largest >= amount - 1 else 0
    given, surplus = [largest] + [least] * (amount - 1), total - largest - least * (amount - 1)
    while surplus > 0:
        movable = [i for i in range(1, amount) if given[i] < largest] or [i for i in range(1, amount) if given[i] < most]
        pool, remaining = sum([weights[i] for i in movable]), surplus
        for i in movable:
            extra = min(most - given[i], max(1, remaining * weights[i] // pool), surplus)
            given[i] = given[i] + extra
            surplus = surplus - extra
    return np.array(given)


def bell_draw(key, extent, deviation, most, shards=(), kind=jnp.bfloat16):
    drawn = deviation * jax.random.normal(key, extent, jnp.float32)
    if shards:
        drawn = drawn * steps_of(key, extent, shards, -0.22, 0.18)
    return jnp.clip(drawn, -most, most).astype(kind)


def heavy_noise(rng, dims, width, bound, shards, heavy, kind=jnp.bfloat16):
    entries = width * jax.random.normal(rng, dims, jnp.float32)
    if shards:
        entries = entries * steps_of(rng, dims, shards, -0.22, 0.18)
    return jnp.clip(with_spikes(entries, jax.random.fold_in(rng, 3), *heavy), -bound, bound).astype(kind)


def setup_inputs(seed: int = 0) -> dict:
    key_of = jax.random.split(jax.random.key(seed), 13)
    tokens = bell_draw(key_of[0], (TOKENS, D), 1.0, 6.0, ((0, 8),))
    cotangent = heavy_noise(key_of[1], (TOKENS, D), 1.0, 6.0, ((0, 32),), (0, 1, 32, 2.75))
    mix_coef = jnp.clip(0.25 + 0.5 * jax.random.uniform(key_of[2], (TOKENS,), jnp.float32) ** steps_of(key_of[2], (TOKENS,), ((0, 32),), -0.2, 0.2), 0.25, 0.75)
    partner_dev_keys = jax.random.split(jax.random.fold_in(key_of[3], 1), TOKENS // QROWS)
    partner_dev_turns = jax.random.permutation(jax.random.fold_in(key_of[3], 3), TOKENS // QROWS)
    partner_dev = jax.vmap(lambda own, number: assign_block(jax.random.fold_in(key_of[3], 2), own, number, QROWS, N_DP, 1, CAP, 1))(partner_dev_keys, partner_dev_turns).reshape((TOKENS, 1))
    partner_row = place_ends(jax.random.randint(key_of[4], (TOKENS,), 0, ROWS_DEV), jax.random.fold_in(key_of[4], 1), 0, ROWS_DEV - 1).astype(jnp.int32)
    view_counts = place_ends(jax.random.randint(key_of[5], (CLIPS, 2), VL // 4, VL + 1), jax.random.fold_in(key_of[5], 1), VL // 4, VL).astype(jnp.int32)
    w_qkv = bell_draw(key_of[6], (2, D, 3, D), D ** -0.5, 0.21875, ((3, 4),))
    w_out = bell_draw(key_of[7], (2, D, D), (max(1, D // 64)) ** -0.5, 1.75, ((1, 4),))
    w_up = bell_draw(key_of[8], (2, D, FF), D ** -0.5, 0.21875, ((2, 4),))
    w_down = bell_draw(key_of[9], (2, FF, D), FF ** -0.5, 0.109375, ((1, 4),))
    gain_attn = jnp.clip(1.0 + 0.18 * jax.random.normal(key_of[10], (2, D), jnp.float32), 0.1, 1.9)
    gain_mlp = jnp.clip(1.0 + 0.18 * jax.random.normal(key_of[11], (2, D), jnp.float32), 0.1, 1.9)
    return {"tokens": tokens, "cotangent": cotangent, "mix_coef": mix_coef, "partner_dev": partner_dev, "partner_row": partner_row, "view_counts": view_counts, "w_qkv": w_qkv, "w_out": w_out, "w_up": w_up, "w_down": w_down, "gain_attn": gain_attn, "gain_mlp": gain_mlp}


epsilon = 1e-06
masked_score = -1000000000.0
highest = lax.Precision.HIGHEST

@jax.custom_vjp
def low(v):
    return lax.optimization_barrier(v.astype(jnp.bfloat16)).astype(jnp.float32)

@jax.custom_vjp
def low_back(v):
    return v

def low_keep(v):
    return (low(v), None)

def low_pass(kept, grad):
    return (grad,)

def back_keep(v):
    return (v, None)

def back_low(kept, grad):
    return (low(grad),)
low.defvjp(low_keep, low_pass)
low_back.defvjp(back_keep, back_low)

def layer_norm(values, gain):
    centred = values - lax.optimization_barrier(jnp.mean(values, axis=-1, keepdims=True))
    spread = lax.optimization_barrier(jnp.mean(centred * centred, axis=-1, keepdims=True))
    return centred * lax.rsqrt(spread + epsilon) * gain

def clip_layer(stream, counts, qkv_weight, out_weight, up_weight, down_weight, attn_gain, mlp_gain, across):
    normed = low(layer_norm(stream, attn_gain))
    projected = low_back(low(jnp.dot(normed, qkv_weight.reshape(D, 3 * D), precision=highest)))
    queries = projected[:, :D].reshape(2, VL, HEADS, HD)
    key_rows = projected[:, D:2 * D].reshape(2, VL, HEADS, HD)
    value_rows = projected[:, 2 * D:].reshape(2, VL, HEADS, HD)
    key_counts = counts
    if across:
        key_rows = key_rows[::-1]
        value_rows = value_rows[::-1]
        key_counts = counts[::-1]
    scores = low_back(jnp.einsum('vqhd,vkhd->vhqk', queries, key_rows, precision=highest) * HD ** (-0.5))
    usable = jnp.arange(VL, dtype=jnp.int32)[None, :] < key_counts[:, None]
    scores = jnp.where(usable[:, None, None, :], scores, masked_score)
    weights = low(jax.nn.softmax(scores, axis=-1))
    attended = jnp.einsum('vhqk,vkhd->vqhd', weights, value_rows, precision=highest)
    attended = low_back(low(attended.reshape(2 * VL, D)))
    stream = stream + low_back(jnp.dot(attended, out_weight, precision=highest))
    hidden = low_back(jnp.dot(low(layer_norm(stream, mlp_gain)), up_weight, precision=highest))
    activated = low(jax.nn.gelu(hidden, approximate=False))
    return stream + low_back(jnp.dot(activated, down_weight, precision=highest))

def reference(tokens, cotangent, mix_coef, partner_dev, partner_row, view_counts, w_qkv, w_out, w_up, w_down, gain_attn, gain_mlp):
    partner = partner_dev[:, 0] * ROWS_DEV + partner_row

    def forward(token_rows, qkv_all, out_all, up_all, down_all, attn_gains, mlp_gains):
        weight_own = mix_coef[:, None]
        mixed = weight_own * token_rows + (1.0 - weight_own) * token_rows[partner]
        stream = mixed.reshape(CLIPS, ROWS_DEV, D)
        for layer_idx in range(2):

            def per_clip(item, layer_idx=layer_idx):
                clip_rows, counts = item
                return clip_layer(clip_rows, counts, qkv_all[layer_idx], out_all[layer_idx], up_all[layer_idx], down_all[layer_idx], attn_gains[layer_idx], mlp_gains[layer_idx], layer_idx == 1)
            stream = lax.map(jax.checkpoint(per_clip), (stream, view_counts))
        return stream.reshape(TOKENS, D)
    inputs = (tokens.astype(jnp.float32), w_qkv.astype(jnp.float32), w_out.astype(jnp.float32), w_up.astype(jnp.float32), w_down.astype(jnp.float32), gain_attn.astype(jnp.float32), gain_mlp.astype(jnp.float32))
    result, pull = jax.vjp(forward, *inputs)
    grads = pull(cotangent.astype(jnp.float32))
    return (result.astype(jnp.bfloat16), grads[0], grads[1], grads[2], grads[3], grads[4], grads[5], grads[6])
```

```python
import jax
import jax.numpy as jnp
from jax import lax
from jax.sharding import PartitionSpec as P

HD = 64
SCALE = HD ** (-0.5)
epsilon = 1e-06
masked_score = -1000000000.0
bf16 = jnp.bfloat16
f32 = jnp.float32


def dot(left, right):
    return jnp.dot(left, right, preferred_element_type=f32)


def dot_rt(left, right):
    return lax.dot_general(left, right, (((1,), (1,)), ((), ())), preferred_element_type=f32)


def dot_lt(left, right):
    return lax.dot_general(left, right, (((0,), (0,)), ((), ())), preferred_element_type=f32)


def swap_core(values):
    return lax.ppermute(values, "mp", [(i, i ^ 1) for i in range(4)])


def swap_view(values):
    return lax.ppermute(values, "mp", [(i, i ^ 2) for i in range(4)])


def with_core(values):
    return jnp.concatenate([values, swap_core(values)], axis=0)


def norm_parts(values):
    centred = values - jnp.mean(values, axis=-1, keepdims=True)
    rstd = lax.rsqrt(jnp.mean(centred * centred, axis=-1, keepdims=True) + epsilon)
    return centred * rstd, rstd


def norm_back(values, gain, upstream):
    n, rstd = norm_parts(values)
    gain_grad = jnp.sum(upstream * n, axis=0)
    dn = upstream * gain
    grad = rstd * (
        dn - jnp.mean(dn, axis=-1, keepdims=True) - n * jnp.mean(dn * n, axis=-1, keepdims=True)
    )
    return grad, gain_grad


def heads_of(values):
    return values.reshape(values.shape[0], -1, HD)


def attend(q, k, v, usable):
    scores = jnp.einsum("qhd,khd->hqk", heads_of(q), heads_of(k), preferred_element_type=f32) * SCALE
    scores = jnp.where(usable[None, None, :], scores, masked_score)
    row_max = jnp.max(scores, axis=-1, keepdims=True)
    exponent = jnp.exp(scores - row_max)
    row_total = jnp.sum(exponent, axis=-1, keepdims=True)
    weights = (exponent / row_total).astype(bf16)
    out = jnp.einsum("hqk,khd->qhd", weights, heads_of(v), preferred_element_type=f32)
    return out.astype(bf16).reshape(q.shape), row_max + jnp.log(row_total)


def attend_back(q, k, v, log_total, grad_out, usable):
    q3, k3, v3, g3 = heads_of(q), heads_of(k), heads_of(v), heads_of(grad_out)
    scores = jnp.einsum("qhd,khd->hqk", q3, k3, preferred_element_type=f32) * SCALE
    scores = jnp.where(usable[None, None, :], scores, masked_score)
    probs = jnp.exp(scores - log_total)
    dv = jnp.einsum("hqk,qhd->khd", probs.astype(bf16), g3, preferred_element_type=f32)
    dp = jnp.einsum("qhd,khd->hqk", g3, v3, preferred_element_type=f32)
    centre = jnp.sum(probs * dp, axis=-1, keepdims=True)
    ds = (probs * (dp - centre)).astype(bf16)
    dq = jnp.einsum("hqk,khd->qhd", ds, k3, preferred_element_type=f32) * SCALE
    dk = jnp.einsum("hqk,qhd->khd", ds, q3, preferred_element_type=f32) * SCALE
    return (
        dq.reshape(q.shape).astype(bf16),
        dk.reshape(q.shape).astype(bf16),
        dv.reshape(q.shape).astype(bf16),
    )


def gelu_parts(hidden):
    phi = 0.5 * lax.erfc(-hidden * (0.5**0.5))
    slope = phi + hidden * jnp.exp(-0.5 * hidden * hidden) * ((2.0 * jnp.pi) ** -0.5)
    return (hidden * phi).astype(bf16), slope


def on_device(
    tokens,
    cotangent,
    mix_coef,
    partner_dev,
    partner_row,
    view_counts,
    w_qkv,
    w_out,
    w_up,
    w_down,
    gain_attn,
    gain_mlp,
):
    peers = lax.axis_size("dp")
    rows = mix_coef.shape[0]
    clip_rows, width = tokens.shape
    mine = w_qkv.shape[-1]
    block = width // peers
    capacity = max(2, 2 * rows // peers)
    slots = peers * capacity
    place = lax.axis_index("mp")
    view = place // 2
    half = place % 2
    counts = view_counts[0]
    side = lax.axis_index("dp") % 2

    qkv_w, out_w = [], []
    for layer in range(2):
        own = w_qkv[layer].reshape(width, 3 * mine)
        other = swap_view(own)
        qkv_w.append(
            jnp.concatenate(
                [own.reshape(width, 3, mine), other.reshape(width, 3, mine)], axis=2
            ).reshape(width, 6 * mine)
        )
        out_w.append(jnp.concatenate([w_out[layer], swap_view(w_out[layer])], axis=0))

    target = partner_dev[:, 0]
    chosen = target[:, None] == jnp.arange(peers, dtype=jnp.int32)[None, :]
    earlier = jnp.arange(rows)[:, None] > jnp.arange(rows)[None, :]
    before = dot(earlier.astype(bf16), chosen.astype(bf16))
    rank = jnp.sum(jnp.where(chosen, before, 0.0), axis=1).astype(jnp.int32)
    slot = target * capacity + rank
    in_slot = slot[:, None] == jnp.arange(slots, dtype=jnp.int32)[None, :]
    requests = jnp.sum(jnp.where(in_slot, partner_row[:, None], 0), axis=0).reshape(peers, capacity)
    pick = in_slot.astype(bf16)
    asked = lax.all_to_all(requests, "dp", split_axis=0, concat_axis=0, tiled=True).reshape(-1)
    clip_index = jnp.arange(clip_rows, dtype=jnp.int32)[None, :]
    found = dot((asked[:, None] == clip_index).astype(bf16), tokens).astype(bf16)
    replies = lax.all_to_all(
        found.reshape(peers, capacity, width), "dp", split_axis=0, concat_axis=0, tiled=True
    )
    partner_tokens = dot(pick, replies.reshape(slots, width))
    own_tokens = lax.dynamic_slice_in_dim(tokens, place * rows, rows, 0)
    weight_own = mix_coef[:, None]
    stream = weight_own * own_tokens.astype(f32) + (1.0 - weight_own) * partner_tokens

    index = jnp.arange(2 * rows, dtype=jnp.int32)
    position = jnp.where(index < rows, index + half * rows, index - half * rows)
    saved = []
    for layer in range(2):
        layer_in = stream
        a_share = (norm_parts(layer_in)[0] * gain_attn[layer]).astype(bf16)
        a_own = with_core(a_share)
        a_key = a_own if layer == 0 else with_core(swap_view(a_share))
        usable = position < (counts[view] if layer == 0 else counts[1 - view])
        q = dot(a_own, qkv_w[layer][:, : 2 * mine]).astype(bf16)
        kv = dot(a_key, qkv_w[layer][:, 2 * mine :]).astype(bf16)
        k, v = kv[:, : 2 * mine], kv[:, 2 * mine :]
        o, log_total = attend(q, k, v, usable)
        part = dot(o, out_w[layer])
        stream = layer_in + part[:rows] + swap_core(part[rows:])
        layer_mid = stream
        b_share = (norm_parts(layer_mid)[0] * gain_mlp[layer]).astype(bf16)
        b_own = with_core(b_share)
        b_far = with_core(swap_view(b_share))
        z_own, slope_own = gelu_parts(dot(b_own, w_up[layer]))
        z_far, slope_far = gelu_parts(dot(b_far, w_up[layer]))
        part_far = dot(z_far, w_down[layer])
        sum_far = part_far[:rows] + swap_core(part_far[rows:])
        arrived = swap_view(sum_far.astype(bf16))
        part = dot(z_own, w_down[layer])
        stream = layer_mid + part[:rows] + swap_core(part[rows:]) + arrived.astype(f32)
        saved.append(
            (layer_in, a_own, a_key, usable, q, k, v, o, log_total, layer_mid)
            + (b_own, b_far, z_own, z_far, slope_own, slope_far)
        )
    layer_output = stream.astype(bf16)

    def over_dp(grads):
        n = grads.shape[1]
        cut = grads.reshape(peers // 2, 2, block, n)
        keep = lax.dynamic_index_in_dim(cut, side, 1, False)
        send = lax.dynamic_index_in_dim(cut, 1 - side, 1, False).astype(bf16)
        got = lax.ppermute(send, "dp", [(i, i ^ 1) for i in range(peers)])
        both = (keep + got.astype(f32)).astype(bf16).reshape(peers // 2 * block, n)
        groups = [list(range(s, peers, 2)) for s in range(2)]
        return lax.psum_scatter(
            both, "dp", scatter_dimension=0, tiled=True, axis_index_groups=groups
        ).astype(f32)

    gradient = cotangent.astype(f32)
    attn_sums = [None, None]
    mlp_sums = [None, None]
    gain_parts = [None] * 4
    for layer in (1, 0):
        (layer_in, a_own, a_key, usable, q, k, v, o, log_total, layer_mid) = saved[layer][:10]
        (b_own, b_far, z_own, z_far, slope_own, slope_far) = saved[layer][10:]
        gm = gradient.astype(bf16)
        g_own = with_core(gm)
        g_far = with_core(swap_view(gm))
        du_own = (dot_rt(g_own, w_down[layer]) * slope_own).astype(bf16)
        du_far = (dot_rt(g_far, w_down[layer]) * slope_far).astype(bf16)
        part_far = dot_rt(du_far, w_up[layer])
        sum_far = part_far[:rows] + swap_core(part_far[rows:])
        arrived = swap_view(sum_far.astype(bf16))
        part = dot_rt(du_own, w_up[layer])
        db = part[:rows] + swap_core(part[rows:]) + arrived.astype(f32)
        grad_up = dot_lt(b_own, du_own) + dot_lt(b_far, du_far)
        grad_down = dot_lt(g_own, z_own) + dot_lt(g_far, z_far)
        mlp_sums[layer] = over_dp(jnp.concatenate([grad_up, grad_down], axis=1))
        dx, gain_parts[2 + layer] = norm_back(layer_mid, gain_mlp[layer], db)
        gradient = gradient + dx

        gy = with_core(gradient.astype(bf16))
        do = dot_rt(gy, out_w[layer]).astype(bf16)
        dq, dk, dv = attend_back(q, k, v, log_total, do, usable)
        dkv = jnp.concatenate([dk, dv], axis=1)
        grad_q = dot_lt(a_own, dq)
        grad_kv = dot_lt(a_key, dkv)
        grad_out = dot_lt(gy, o)
        pieces = [grad_q, grad_kv[:, : 2 * mine], grad_kv[:, 2 * mine :], grad_out]
        near = jnp.concatenate([piece[:, :mine] for piece in pieces], axis=1)
        far = jnp.concatenate([piece[:, mine:] for piece in pieces], axis=1)
        attn_sums[layer] = over_dp(near + swap_view(far.astype(bf16)).astype(f32))
        wq, wkv = qkv_w[layer][:, : 2 * mine], qkv_w[layer][:, 2 * mine :]
        if layer == 0:
            part = dot_rt(jnp.concatenate([dq, dkv], axis=1), qkv_w[layer])
            da = part[:rows] + swap_core(part[rows:])
        else:
            part_far = dot_rt(dkv, wkv)
            sum_far = part_far[:rows] + swap_core(part_far[rows:])
            arrived = swap_view(sum_far.astype(bf16))
            part = dot_rt(dq, wq)
            da = part[:rows] + swap_core(part[rows:]) + arrived.astype(f32)
        dx, gain_parts[layer] = norm_back(layer_in, gain_attn[layer], da)
        gradient = gradient + dx

    outgoing = dot_lt(pick, ((1.0 - weight_own) * gradient).astype(bf16)).astype(bf16)
    gains = jnp.stack(gain_parts).reshape(4, peers, block).transpose(1, 0, 2).reshape(peers, 4 * block)
    high = gains.astype(bf16)
    low = (gains - high.astype(f32)).astype(bf16)
    extra = jnp.concatenate([high, low], axis=1)
    extra = jnp.pad(extra, ((0, 0), (0, width - 8 * block)))
    extra = jnp.pad(extra[:, None, :], ((0, 0), (0, 7), (0, 0)))
    outgoing = jnp.concatenate([outgoing.reshape(peers, capacity, width), extra], axis=1)
    returned = lax.all_to_all(outgoing, "dp", split_axis=0, concat_axis=0, tiled=True)
    gain_row = jnp.sum(returned[:, capacity, : 8 * block].astype(f32), axis=0)
    gain_sum = gain_row[: 4 * block] + gain_row[4 * block :]
    gain_sum = gain_sum + swap_core(gain_sum)
    gain_sum = (gain_sum + swap_view(gain_sum)).reshape(4, block)
    returned = returned[:, :capacity].reshape(slots, width)
    nearby = ((asked // rows) ^ place) * rows + asked % rows
    spread = dot_lt((nearby[:, None] == clip_index).astype(bf16), returned)
    sum_far = spread[2 * rows : 3 * rows] + swap_core(spread[3 * rows :])
    arrived = swap_view(sum_far.astype(bf16))
    partner_grad = spread[:rows] + swap_core(spread[rows : 2 * rows]) + arrived.astype(f32)
    grad_tokens = weight_own * gradient + partner_grad

    attn = jnp.stack(attn_sums)
    mlp = jnp.stack(mlp_sums)
    hidden = mlp.shape[-1] // 2
    return (
        layer_output,
        grad_tokens,
        attn[:, :, : 3 * mine].reshape(2, block, 3, mine),
        attn[:, :, 3 * mine :].transpose(0, 2, 1),
        mlp[:, :, :hidden],
        mlp[:, :, hidden:].transpose(0, 2, 1),
        gain_sum[:2],
        gain_sum[2:],
    )


def solution(mesh):
    placed = (
        P("dp", None),
        P(("dp", "mp"), None),
        P(("dp", "mp")),
        P(("dp", "mp"), None),
        P(("dp", "mp")),
        P("dp", None),
        P(None, None, None, "mp"),
        P(None, "mp", None),
        P(None, None, "mp"),
        P(None, "mp", None),
        P(),
        P(),
    )
    return jax.shard_map(
        on_device,
        mesh=mesh,
        in_specs=placed,
        out_specs=(
            P(("dp", "mp"), None),
            P(("dp", "mp"), None),
            P(None, "dp", None, "mp"),
            P(None, "mp", "dp"),
            P(None, "dp", "mp"),
            P(None, "mp", "dp"),
            P(None, "dp"),
            P(None, "dp"),
        ),
        check_vma=False,
    )
```

```python
import functools

import jax
import jax.numpy as jnp
from jax import lax
from jax.experimental import pallas as pl
from jax.experimental.pallas import tpu as pltpu
from jax.sharding import PartitionSpec as P

HD = 64
SCALE = HD ** (-0.5)
epsilon = 1e-06
masked_score = -1000000000.0
bf16 = jnp.bfloat16
f32 = jnp.float32
i32 = jnp.int32

TAIL_P = 0.38
TAIL = (
    0.2144098248509563,
    0.21394460416600933,
    0.20368405029440034,
    0.13968567743708352,
    0.2272053511927878,
    -0.15681775904774625,
    0.3593185352386043,
    -0.25984971762641107,
    0.058419421394547984,
)


def dot(left, right):
    return jnp.dot(left, right, preferred_element_type=f32)


def dot_rt(left, right):
    return lax.dot_general(left, right, (((1,), (1,)), ((), ())), preferred_element_type=f32)


def dot_lt(left, right):
    return lax.dot_general(left, right, (((0,), (0,)), ((), ())), preferred_element_type=f32)


def swap_core(values):
    return lax.ppermute(values, "mp", [(i, i ^ 1) for i in range(4)])


def swap_view(values):
    return lax.ppermute(values, "mp", [(i, i ^ 2) for i in range(4)])


def swap_side(values):
    return lax.ppermute(values, "dp", [(i, i ^ 1) for i in range(lax.axis_size("dp"))])


def after(values, *others):
    return lax.optimization_barrier((values, *others))[0]


def run(body, outs, args, us=1.0, scalars=(), scratch=()):
    return pl.pallas_call(
        body,
        out_shape=[jax.ShapeDtypeStruct(s, d) for s, d in outs],
        in_specs=[
            pl.BlockSpec(memory_space=pltpu.SMEM if i in scalars else pltpu.VMEM)
            for i in range(len(args))
        ],
        out_specs=[pl.BlockSpec(memory_space=pltpu.VMEM) for _ in outs],
        scratch_shapes=list(scratch),
        compiler_params=pltpu.CompilerParams(vmem_limit_bytes=VMEM_LIMIT),
        cost_estimate=pl.CostEstimate(
            flops=int(us * PEAK), bytes_accessed=0, transcendentals=0
        ),
    )(*args)


VMEM_LIMIT = 16 * 1024 * 1024
PEAK = 1


def norm_parts(values):
    centred = values - jnp.mean(values, axis=-1, keepdims=True)
    rstd = lax.rsqrt(jnp.mean(centred * centred, axis=-1, keepdims=True) + epsilon)
    return centred * rstd, rstd


def join_body(count, *refs):
    base, terms, gain = refs[0], refs[1 : 1 + count], refs[1 + count]
    total = base[...]
    for term in terms:
        total = total + term[...].astype(f32)
    refs[2 + count][...] = total
    refs[3 + count][...] = (norm_parts(total)[0] * gain[...]).astype(bf16)


def join_norm(base, terms, gain):
    outs = [(base.shape, f32), (base.shape, bf16)]
    body = functools.partial(join_body, len(terms))
    return run(body, outs, (base, *terms, gain[None]), us=1.1)


def norm_back_body(count, *refs):
    values, gain, gradient = refs[:3]
    total = refs[3][...].astype(f32)
    for term in refs[4 : 3 + count]:
        total = total + term[...].astype(f32)
    n, rstd = norm_parts(values[...])
    refs[3 + count][...] = jnp.sum(total * n, axis=0, keepdims=True)
    dn = total * gain[...]
    dx = rstd * (
        dn - jnp.mean(dn, axis=-1, keepdims=True) - n * jnp.mean(dn * n, axis=-1, keepdims=True)
    )
    new = gradient[...].astype(f32) + dx
    refs[4 + count][...] = new
    refs[5 + count][...] = new.astype(bf16)


def norm_back(values, gain, gradient, terms):
    outs = [((1, values.shape[1]), f32), (values.shape, f32), (values.shape, bf16)]
    body = functools.partial(norm_back_body, len(terms))
    return run(body, outs, (values, gain[None], gradient, *terms), us=1.5)


def finish_body(s0, s1, qkv, out):
    m = out.shape[1]
    for layer, ref in enumerate((s0, s1)):
        for i in range(3):
            qkv[layer, i] = ref[:, i * m : (i + 1) * m].astype(f32)
        out[layer] = ref[:, 3 * m :].astype(f32).T


def ask_body(capacity, target, partner, slot_ref, ask_ref):
    peers = ask_ref.shape[0]
    rows = target.shape[1]
    chosen = lax.broadcasted_iota(i32, (peers, rows), 0) == target[...]
    earlier = lax.broadcasted_iota(i32, (rows, rows), 0) < lax.broadcasted_iota(
        i32, (rows, rows), 1
    )
    before = dot(jnp.where(chosen, 1.0, 0.0).astype(bf16), jnp.where(earlier, 1.0, 0.0).astype(bf16))
    rank = jnp.sum(jnp.where(chosen, before, 0.0), axis=0, keepdims=True).astype(i32)
    slot_ref[...] = target[...] * capacity + rank
    placed = lax.broadcasted_iota(i32, (capacity, rows), 0) == rank
    placed = jnp.where(placed, 1.0, 0.0).astype(bf16)
    high = partner[...] // 32
    low = partner[...] - high * 32
    part = lambda v: dot_rt(jnp.where(chosen, v.astype(f32), 0.0).astype(bf16), placed)
    ask_ref[...] = (part(high) * 32.0 + part(low)).astype(i32)


def one_hot(index, count):
    hit = lax.broadcasted_iota(i32, (count, index.shape[1]), 0) == index[...]
    return jnp.where(hit, 1.0, 0.0).astype(bf16)


def find_body(asked, tokens, found):
    found[...] = dot_lt(one_hot(asked, tokens.shape[0]), tokens[...]).astype(bf16)


def mix_body(slot, replies, own, weight, gain, stream, normed):
    partner = dot_lt(one_hot(slot, replies.shape[0]), replies[...])
    total = weight[...] * own[...].astype(f32) + (1.0 - weight[...]) * partner
    stream[...] = total
    normed[...] = (norm_parts(total)[0] * gain[...]).astype(bf16)


def give_body(slot, weight, gradient, g0, g1, g2, g3, outgoing):
    peers, count, _ = outgoing.shape
    capacity = count - 8
    rows = ((1.0 - weight[...]) * gradient[...]).astype(bf16)
    placed = dot(one_hot(slot, peers * capacity), rows).astype(bf16)
    gains = jnp.concatenate([g0[...], g1[...], g2[...], g3[...]], axis=0)
    high = gains.astype(bf16)
    extra = jnp.concatenate([high.astype(f32), gains - high.astype(f32)], axis=0).astype(bf16)
    for p in range(peers):
        outgoing[p, :capacity, :] = placed[p * capacity : (p + 1) * capacity, :]
        outgoing[p, capacity:, :] = extra


def spread_body(place, asked, returned, gains, *refs):
    near, core, far, far_core, flat = refs
    peers, count, _ = returned.shape
    capacity = count - 8
    rows = near.shape[0]
    total = jnp.zeros((8, near.shape[1]), f32)
    for p in range(peers):
        flat[p * capacity : (p + 1) * capacity, :] = returned[p, :capacity, :]
        total = total + returned[p, capacity:, :].astype(f32)
    gains[...] = total[:4] + total[4:]
    for i, ref in enumerate((near, core, far, far_core)):
        owner = jnp.bitwise_xor(place[0], i)
        ref[...] = dot(one_hot(asked[...] - owner * rows, rows), flat[...])


def gelu_parts(u):
    t = 1.0 / (1.0 + (TAIL_P * 0.5**0.5) * jnp.abs(u))
    poly = TAIL[-1]
    for c in TAIL[-2::-1]:
        poly = poly * t + c
    bell = jnp.exp(-0.5 * u * u)
    tail = 0.5 * poly * t * bell
    phi = jnp.where(u < 0.0, tail, 1.0 - tail)
    return u * phi, phi + u * bell * 0.3989422804014327


def mlp_body(layer, b0, b1, up, down, saved, slope, p0, p1):
    rows, width = b0.shape
    b = jnp.concatenate([b0[...], b1[...]], axis=0)
    saved[:, :width] = b
    for j in range(0, up.shape[2], 256):
        z, dz = gelu_parts(dot(b, up[layer, :, j : j + 256]))
        saved[:, width + j : width + j + 256] = z.astype(bf16)
        slope[:, j : j + 256] = dz
    p0[...] = dot(saved[:rows, width:], down[layer])
    p1[...] = dot(saved[rows:, width:], down[layer])


def mlp(layer, b, up, down):
    rows, width = b[0].shape
    hidden = up.shape[2]
    outs = [((2 * rows, width + hidden), bf16), ((2 * rows, hidden), f32)]
    outs += [((rows, width), f32)] * 2
    body = functools.partial(mlp_body, layer)
    return run(body, outs, (*b, up, down), us=3.5)


def mlp_back_body(layer, g0, g1, slope, up, down, saved, p0, p1):
    rows, width = g0.shape
    g = jnp.concatenate([g0[...], g1[...]], axis=0)
    saved[:, :width] = g
    for j in range(0, up.shape[2], 256):
        dz = dot_rt(g, down[layer, j : j + 256, :])
        saved[:, width + j : width + j + 256] = (dz * slope[:, j : j + 256]).astype(bf16)
    p0[...] = dot_rt(saved[:rows, width:], up[layer])
    p1[...] = dot_rt(saved[rows:, width:], up[layer])


def mlp_back(layer, g, slope, up, down):
    rows, width = g[0].shape
    hidden = up.shape[2]
    outs = [((2 * rows, width + hidden), bf16)] + [((rows, width), f32)] * 2
    body = functools.partial(mlp_back_body, layer)
    return run(body, outs, (*g, slope, up, down), us=2.5)


def cut_rows(side, values, send, keep, column):
    count, block, _ = send.shape
    n = values.shape[1]
    for z in range(count):
        theirs = pl.multiple_of((2 * z + 1 - side[0]) * block, 8)
        mine = pl.multiple_of((2 * z + side[0]) * block, 8)
        send[z, :, column : column + n] = values[pl.ds(theirs, block), :].astype(bf16)
        keep[z, :, column : column + n] = values[pl.ds(mine, block), :]


def mlp_sums_body(own, far, own_g, far_g, sums):
    hidden = sums.shape[1] // 2
    width = own.shape[1] - hidden
    for i in range(2):
        left = (own, far) if i == 0 else (own_g, far_g)
        right = (own_g, far_g) if i == 0 else (own, far)
        left = jnp.concatenate([v[:, :width] for v in left], axis=0)
        right = jnp.concatenate([v[:, width:] for v in right], axis=0)
        sums[:, i * hidden : (i + 1) * hidden] = dot_lt(left, right).astype(bf16)


def mlp_sums(width, own, far, own_g, far_g):
    outs = [((width, 2 * (own.shape[1] - width)), bf16)]
    return run(mlp_sums_body, outs, (own, far, own_g, far_g), us=3.5)[0]


def cut_outside(side, peers, grads):
    parts = grads.reshape(peers // 2, 2, -1, grads.shape[1])
    send = lax.dynamic_index_in_dim(parts, 1 - side[0], 1, False)
    return send.astype(bf16), lax.dynamic_index_in_dim(parts, side[0], 1, False)


def groups_of(n):
    return [(j, min(128, n - j)) for j in range(0, n, 128)]


def places(width, n):
    stride = -(-n // 128) * 128
    return [width + i * stride for i in range(5)]


def key_bias(rows, half, count):
    index = lax.broadcasted_iota(i32, (2 * rows, 1), 0)
    position = jnp.where(index < rows, index + half * rows, index - half * rows)
    return jnp.where(position < count, 0.0, masked_score).astype(f32)


def masked(values, head):
    if values.shape[1] == HD:
        return values
    keep = lax.broadcasted_iota(i32, values.shape, 1) // HD == head
    return jnp.where(keep, values, jnp.zeros_like(values))


def attend_core(from_q, from_k, lse, bias, width, n):
    q0, k0, v0, o0, _ = places(width, n)
    lse[...] = jnp.zeros(lse.shape, f32)
    for j, w in groups_of(n):
        q = from_q[:, q0 + j : q0 + j + w] * jnp.asarray(SCALE, bf16)
        k = from_k[:, k0 + j : k0 + j + w]
        v = from_k[:, v0 + j : v0 + j + w]
        out = jnp.zeros((w, q.shape[0]), f32)
        for head in range(w // HD):
            s = dot_rt(k, masked(q, head)) + bias
            top = jnp.max(s, axis=0, keepdims=True)
            e = jnp.exp(s - top)
            total = jnp.sum(e, axis=0, keepdims=True)
            weights = (e * (1.0 / total)).astype(bf16)
            at = j // HD + head
            lse[at : at + 1, :] = top + jnp.log(total)
            out = out + dot_lt(masked(v, head), weights)
        from_q[:, o0 + j : o0 + j + w] = out.T.astype(bf16)


def attend_back_core(from_q, from_k, do, lse, bias, back, width, n):
    q0, k0, v0, _, _ = places(width, n)
    for j, w in groups_of(n):
        q = from_q[:, q0 + j : q0 + j + w] * jnp.asarray(SCALE, bf16)
        k = from_k[:, k0 + j : k0 + j + w]
        v = from_k[:, v0 + j : v0 + j + w]
        d = do[:, j : j + w]
        dv = jnp.zeros(q.shape, f32)
        dk = jnp.zeros(q.shape, f32)
        dq = jnp.zeros((w, q.shape[0]), f32)
        for head in range(w // HD):
            qm, dm, km = masked(q, head), masked(d, head), masked(k, head)
            at = j // HD + head
            p = jnp.exp(dot_rt(k, qm) + bias - lse[at : at + 1, :])
            dp = dot_rt(v, dm)
            centre = jnp.sum(p * dp, axis=0, keepdims=True)
            ds = (p * (dp - centre)).astype(bf16)
            dv = dv + dot(p.astype(bf16), dm)
            dk = dk + dot(ds, qm)
            dq = dq + dot_lt(km, ds)
        back[:, q0 + j : q0 + j + w] = (dq.T * SCALE).astype(bf16)
        back[:, k0 + j : k0 + j + w] = dk.astype(bf16)
        back[:, v0 + j : v0 + j + w] = dv.astype(bf16)


def join_weights(own, far, own_o, far_o, w, wo):
    m = own_o.shape[1]
    for i in range(3):
        w[2 * i * m : (2 * i + 1) * m, :] = own[0, i]
        w[(2 * i + 1) * m : (2 * i + 2) * m, :] = far[0, i]
    wo[:m, :] = own_o[0]
    wo[m:, :] = far_o[0]


def attend_body(info, a0, a1, own, far, own_o, far_o, saved, lse, p0, p1, w, wo):
    join_weights(own, far, own_o, far_o, w, wo)
    rows, width = p0.shape
    n = wo.shape[0]
    q0, _, _, o0, _ = places(width, n)
    a = jnp.concatenate([a0[...], a1[...]], axis=0)
    saved[:, :width] = a
    saved[:, q0:o0] = dot_rt(a, w[...]).astype(bf16)
    attend_core(saved, saved, lse, key_bias(rows, info[0], info[1]), width, n)
    p0[...] = dot(saved[:rows, o0:], wo[...])
    p1[...] = dot(saved[rows:, o0:], wo[...])


def attend(info, shares, weights):
    rows, width = shares[0].shape
    n = 2 * weights[2].shape[1]
    outs = [((2 * rows, width + 4 * n), bf16), ((8, 2 * rows), f32)]
    outs += [((rows, width), f32)] * 2
    scratch = [pltpu.VMEM((3 * n, width), bf16), pltpu.VMEM((n, width), bf16)]
    return run(
        attend_body, outs, (info, *shares, *weights), us=6.5, scalars=(0,), scratch=scratch
    )


def attend_back_body(info, g0, g1, saved, lse, own, far, own_o, far_o, back, p0, p1, do, w, wo):
    join_weights(own, far, own_o, far_o, w, wo)
    rows, width = g0.shape
    n = wo.shape[0]
    g = jnp.concatenate([g0[...], g1[...]], axis=0)
    back[:, :width] = g
    do[...] = dot_rt(g, wo[...]).astype(bf16)
    bias = key_bias(rows, info[0], info[1])
    attend_back_core(saved, saved, do, lse, bias, back, width, n)
    p0[...] = dot(back[:rows, width:], w[...])
    p1[...] = dot(back[rows:, width:], w[...])


def attend_back(info, g, saved, lse, weights):
    rows, width = g[0].shape
    n = 2 * weights[2].shape[1]
    return run(
        attend_back_body,
        [((2 * rows, width + 3 * n), bf16)] + [((rows, width), f32)] * 2,
        (info, *g, saved, lse, *weights),
        us=8.0,
        scalars=(0,),
        scratch=[
            pltpu.VMEM((2 * rows, n), bf16),
            pltpu.VMEM((3 * n, width), bf16),
            pltpu.VMEM((n, width), bf16),
        ],
    )


def attend_sums_body(cut, side, saved, back, near, far, *refs):
    total = refs[-1]
    width, n = near.shape
    m = n // 2
    q0, k0, v0, o0, _ = places(width, n)
    a = saved[:, :width]
    for i in range(2):
        part = dot_lt(a, back[:, q0 + i * n : q0 + (i + 1) * n])
        near[:, i * m : (i + 1) * m] = part[:, :m]
        far[:, i * m : (i + 1) * m] = part[:, m:].astype(bf16)
    for i in range(2):
        if i == 0:
            part = dot_lt(a, back[:, v0 : v0 + n])
        else:
            part = dot_lt(back[:, :width], saved[:, o0 : o0 + n])
        total[:, i * m : (i + 1) * m] = part[:, :m]
        total[:, n + i * m : n + (i + 1) * m] = part[:, m:]
    if cut:
        cut_rows(side, total, refs[0], refs[1], 0)


def attend_sums(side, peers, width, saved, back):
    n = (saved.shape[1] - width) // 4
    block = width // peers
    cut = block % 16 == 0
    outs = [((width, n), f32), ((width, n), bf16)]
    scratch = []
    if cut:
        outs += [((peers // 2, block, 2 * n), bf16), ((peers // 2, block, 2 * n), f32)]
        scratch = [pltpu.VMEM((width, 2 * n), f32)]
    else:
        outs += [((width, 2 * n), f32)]
    out = run(
        functools.partial(attend_sums_body, cut),
        outs,
        (side, saved, back),
        us=3.0,
        scalars=(0,),
        scratch=scratch,
    )
    return out if cut else (*out[:2], *cut_outside(side, peers, out[2]))


def cross_body(info, a0, a1, a2, a3, w, wo, own, far, lse, lse_far, p0, p1, p2, p3):
    rows, width = p0.shape
    n = wo.shape[1]
    q0, k0, v0, o0, _ = places(width, n)
    for saved, halves in ((own, (a0, a1)), (far, (a2, a3))):
        a = jnp.concatenate([halves[0][...], halves[1][...]], axis=0)
        saved[:, :width] = a
        for i, at in enumerate((q0, k0, v0)):
            saved[:, at : at + n] = dot_rt(a, w[1, i]).astype(bf16)
    attend_core(far, own, lse_far, key_bias(rows, info[0], info[1]), width, n)
    p2[...] = dot(far[:rows, o0 : o0 + n], wo[1])
    p3[...] = dot(far[rows:, o0 : o0 + n], wo[1])
    attend_core(own, far, lse, key_bias(rows, info[0], info[2]), width, n)
    p0[...] = dot(own[:rows, o0 : o0 + n], wo[1])
    p1[...] = dot(own[rows:, o0 : o0 + n], wo[1])


def cross(info, shares, w, wo):
    rows, width = shares[0].shape
    wide = places(width, wo.shape[1])[4]
    outs = [((2 * rows, wide), bf16)] * 2 + [((8, 2 * rows), f32)] * 2
    outs += [((rows, width), f32)] * 4
    return run(cross_body, outs, (info, *shares, w, wo), us=6.5, scalars=(0,))


def cross_back_body(which, info, g0, g1, from_q, from_k, lse, wo, back, do):
    rows, width = g0.shape
    n = wo.shape[1]
    g = jnp.concatenate([g0[...], g1[...]], axis=0)
    back[:, :width] = g
    do[...] = dot_rt(g, wo[1]).astype(bf16)
    bias = key_bias(rows, info[0], info[which])
    attend_back_core(from_q, from_k, do, lse, bias, back, width, n)


def cross_back(which, info, g, from_q, from_k, lse, wo):
    rows, width = g[0].shape
    n = wo.shape[1]
    return run(
        functools.partial(cross_back_body, which),
        [((2 * rows, places(width, n)[3]), bf16)],
        (info, *g, from_q, from_k, lse, wo),
        us=4.0,
        scalars=(0,),
        scratch=[pltpu.VMEM((2 * rows, n), bf16)],
    )[0]


def cross_rows_body(own, far, w, p0, p1, p2, p3):
    rows, width = p0.shape
    n = w.shape[2]
    q0, k0, v0, _, _ = places(width, n)
    for queries, keys, parts in ((far, own, (p2, p3)), (own, far, (p0, p1))):
        for i, part in enumerate(parts):
            at = slice(i * rows, (i + 1) * rows)
            part[...] = (
                dot(queries[at, q0 : q0 + n], w[1, 0])
                + dot(keys[at, k0 : k0 + n], w[1, 1])
                + dot(keys[at, v0 : v0 + n], w[1, 2])
            )


def cross_rows(rows, width, own, far, w):
    return run(cross_rows_body, [((rows, width), f32)] * 4, (own, far, w), us=2.0)


def cross_sums_body(own, far, own_back, far_back, sums):
    width = sums.shape[0]
    n = sums.shape[1] // 4
    q0, k0, v0, o0, _ = places(width, n)
    rows = lambda first, second, at, size: jnp.concatenate(
        [first[:, at : at + size], second[:, at : at + size]], axis=0
    )
    queries = rows(own, far, 0, width)
    keys = rows(far, own, 0, width)
    parts = [
        (queries, rows(own_back, far_back, q0, n)),
        (keys, rows(own_back, far_back, k0, n)),
        (keys, rows(own_back, far_back, v0, n)),
        (rows(own_back, far_back, 0, width), rows(own, far, o0, n)),
    ]
    for i, (left, right) in enumerate(parts):
        sums[:, i * n : (i + 1) * n] = dot_lt(left, right).astype(bf16)


def cross_sums(width, n, own, far, own_back, far_back):
    return run(
        cross_sums_body, [((width, 4 * n), bf16)], (own, far, own_back, far_back), us=3.0
    )[0]


def on_device(
    tokens,
    cotangent,
    mix_coef,
    partner_dev,
    partner_row,
    view_counts,
    w_qkv,
    w_out,
    w_up,
    w_down,
    gain_attn,
    gain_mlp,
):
    peers = lax.axis_size("dp")
    rows = mix_coef.shape[0]
    width = tokens.shape[1]
    mine = w_qkv.shape[-1]
    block = width // peers
    capacity = max(2, 2 * rows // peers)
    slots = peers * capacity
    place = lax.axis_index("mp").astype(i32)
    view, half = place // 2, place % 2
    counts = view_counts[0]
    side = (lax.axis_index("dp") % 2).astype(i32)[None]
    weight_own = mix_coef[:, None]

    slot, requests = run(
        functools.partial(ask_body, capacity),
        [((1, rows), i32), ((peers, capacity), i32)],
        (partner_dev.reshape(1, rows), partner_row.reshape(1, rows)),
    )

    own_w = w_qkv.transpose(0, 2, 3, 1)
    far_o = swap_view(w_out[:1])
    far_w = swap_view(own_w[:1])
    asked = lax.all_to_all(requests, "dp", split_axis=0, concat_axis=0, tiled=True)
    asked = after(asked, far_o).reshape(1, slots)
    (found,) = run(find_body, [((slots, width), bf16)], (asked, tokens), us=2.0)
    replies = lax.all_to_all(
        found.reshape(peers, capacity, width), "dp", split_axis=0, concat_axis=0, tiled=True
    )
    own_tokens = lax.dynamic_slice_in_dim(tokens, place * rows, rows, 0)
    replies, far_w, own_tokens = lax.optimization_barrier((replies, far_w, own_tokens))
    stream, a_share = run(
        mix_body,
        [((rows, width), f32), ((rows, width), bf16)],
        (slot, replies.reshape(slots, width), own_tokens, weight_own, gain_attn[:1]),
        us=1.5,
    )
    def feed_forward(layer, b_share):
        b_far = swap_view(b_share)
        own, slope_own, part, part_core = mlp(layer, (b_share, swap_core(b_share)), w_up, w_down)
        b_far = after(b_far, part)
        far, slope_far, there, there_core = mlp(layer, (b_far, swap_core(b_far)), w_up, w_down)
        arrived = swap_view((there + swap_core(there_core)).astype(bf16))
        return (own, far), (slope_own, slope_far), (part, swap_core(part_core), arrived)

    def feed_forward_back(layer, g_share, kept, slope):
        g_far = swap_view(g_share)
        own_g, part, part_core = mlp_back(
            layer, (g_share, swap_core(g_share)), slope[0], w_up, w_down
        )
        g_far = after(g_far, part)
        far_g, there, there_core = mlp_back(layer, (g_far, swap_core(g_far)), slope[1], w_up, w_down)
        arrived = swap_view((there + swap_core(there_core)).astype(bf16))
        sums = mlp_sums(width, *kept, own_g, far_g)
        return sums, (part, swap_core(part_core), after(arrived, sums))

    first_in = stream
    info = jnp.stack([half, counts[view]])
    weights = (own_w[:1], far_w, w_out[:1], far_o)
    kept0, lse0, part, part_core = attend(info, (a_share, swap_core(a_share)), weights)
    first_mid, b_share = join_norm(first_in, (part, swap_core(part_core)), gain_mlp[0])
    mlp0, slope0, terms = feed_forward(0, b_share)

    second_in, a_share = join_norm(first_mid, terms, gain_attn[1])
    a_far = swap_view(a_share)
    shares = (a_share, swap_core(a_share), a_far, swap_core(a_far))
    info1 = jnp.stack([half, counts[view], counts[1 - view]])
    own1, far1, lse1, lse1_far, part, part_core, there, there_core = cross(
        info1, shares, own_w, w_out
    )
    arrived = swap_view((there + swap_core(there_core)).astype(bf16))
    second_mid, b_share = join_norm(second_in, (part, swap_core(part_core), arrived), gain_mlp[1])
    mlp1, slope1, terms = feed_forward(1, b_share)
    layer_output = (second_mid + terms[0] + terms[1] + terms[2].astype(f32)).astype(bf16)

    def along_z(values):
        groups = [list(range(s, peers, 2)) for s in range(2)]
        return lax.psum_scatter(
            values, "dp", scatter_dimension=0, tiled=True, axis_index_groups=groups
        )

    def between_sides(values):
        send = lax.dynamic_slice_in_dim(values, (1 - side[0]) * block, block, 0)
        keep = lax.dynamic_slice_in_dim(values, side[0] * block, block, 0)
        return keep.astype(f32) + swap_side(send).astype(f32)

    gain_parts = [None] * 4
    mlp_sum1, terms = feed_forward_back(1, cotangent, mlp1, slope1)
    sum_mlp1 = along_z(mlp_sum1)
    gain_parts[3], gradient, g_share = norm_back(second_mid, gain_mlp[1], cotangent, terms)

    g_far = swap_view(g_share)
    own_back = cross_back(2, info1, (g_share, swap_core(g_share)), own1, far1, lse1, w_out)
    g_far = after(g_far, own_back)
    far_back = cross_back(1, info1, (g_far, swap_core(g_far)), far1, own1, lse1_far, w_out)
    part, part_core, there, there_core = cross_rows(rows, width, own_back, far_back, own_w)
    arrived = swap_view((there + swap_core(there_core)).astype(bf16))
    attn_sum1 = cross_sums(width, mine, own1, far1, own_back, far_back)
    terms = (part, swap_core(part_core), after(arrived, attn_sum1))
    attn_sum1 = along_z(after(attn_sum1, sum_mlp1))
    gain_parts[1], gradient, g_share = norm_back(second_in, gain_attn[1], gradient, terms)

    mlp_sum0, terms = feed_forward_back(0, g_share, mlp0, slope0)
    sum_mlp0 = along_z(after(mlp_sum0, attn_sum1))
    gain_parts[2], gradient, g_share = norm_back(first_mid, gain_mlp[0], gradient, terms)

    back, part, part_core = attend_back(info, (g_share, swap_core(g_share)), kept0, lse0, weights)
    near, far, send, keep = attend_sums(side, peers, width, kept0, back)
    gain_parts[0], gradient, _ = norm_back(
        first_in, gain_attn[0], gradient, (part, swap_core(part_core))
    )

    (outgoing,) = run(
        give_body,
        [((peers, capacity + 8, width), bf16)],
        (slot, weight_own, gradient, *gain_parts),
        us=1.5,
    )
    returned = lax.all_to_all(outgoing, "dp", split_axis=0, concat_axis=0, tiled=True)

    send_qk, keep_qk = cut_outside(side, peers, near + swap_view(far).astype(f32))
    keep_vo = keep + swap_side(send).astype(f32)
    n = near.shape[1]
    sum_qk = (keep_qk + swap_side(send_qk).astype(f32)).astype(bf16)
    sum_vo = (keep_vo[:, :, :n] + swap_view(keep_vo[:, :, n:].astype(bf16)).astype(f32)).astype(bf16)
    joined = jnp.concatenate([sum_qk, sum_vo], axis=2).reshape(peers // 2 * block, 4 * mine)
    attn_sum0 = along_z(after(joined, sum_mlp0))
    attn_sum1 = between_sides(attn_sum1)
    mlp_all = jnp.stack([between_sides(sum_mlp0), between_sides(sum_mlp1)])
    gain_sum, part, part_core, there, there_core = run(
        spread_body,
        [((4, width), f32)] + [((rows, width), f32)] * 4,
        (place[None], asked, returned),
        us=1.5,
        scalars=(0,),
        scratch=[pltpu.VMEM((slots, width), bf16)],
    )
    gain_sum = gain_sum + swap_core(gain_sum)
    gain_sum = gain_sum + swap_view(gain_sum)
    gain_sum = lax.dynamic_slice_in_dim(gain_sum, lax.axis_index("dp") * block, block, 1)
    arrived = swap_view((there + swap_core(there_core)).astype(bf16))
    grad_tokens = weight_own * gradient + part + swap_core(part_core) + arrived.astype(f32)

    grad_qkv, grad_out = run(
        finish_body, [((2, 3, block, mine), f32), ((2, mine, block), f32)], (attn_sum0, attn_sum1)
    )
    hidden = mlp_all.shape[-1] // 2
    return (
        layer_output,
        grad_tokens,
        grad_qkv.transpose(0, 2, 1, 3),
        grad_out,
        mlp_all[:, :, :hidden],
        mlp_all[:, :, hidden:].transpose(0, 2, 1),
        gain_sum[:2],
        gain_sum[2:],
    )


def solution(mesh):
    placed = (
        P("dp", None),
        P(("dp", "mp"), None),
        P(("dp", "mp")),
        P(("dp", "mp"), None),
        P(("dp", "mp")),
        P("dp", None),
        P(None, None, None, "mp"),
        P(None, "mp", None),
        P(None, None, "mp"),
        P(None, "mp", None),
        P(),
        P(),
    )
    return jax.shard_map(
        on_device,
        mesh=mesh,
        in_specs=placed,
        out_specs=(
            P(("dp", "mp"), None),
            P(("dp", "mp"), None),
            P(None, "dp", None, "mp"),
            P(None, "mp", "dp"),
            P(None, "dp", "mp"),
            P(None, "mp", "dp"),
            P(None, "dp"),
            P(None, "dp"),
        ),
        check_vma=False,
    )
```

```python
import functools

import jax
import jax.numpy as jnp
from jax import lax
from jax.experimental import pallas as pl
from jax.experimental.pallas import tpu as pltpu
from jax.sharding import PartitionSpec as P

HD = 64
SCALE = HD ** (-0.5)
epsilon = 1e-06
masked_score = -1000000000.0
bf16 = jnp.bfloat16
f32 = jnp.float32
i32 = jnp.int32

TAIL_P = 0.38
TAIL = (
    0.2144098248509563,
    0.21394460416600933,
    0.20368405029440034,
    0.13968567743708352,
    0.2272053511927878,
    -0.15681775904774625,
    0.3593185352386043,
    -0.25984971762641107,
    0.058419421394547984,
)


def dot(left, right):
    return jnp.dot(left, right, preferred_element_type=f32)


def dot_rt(left, right):
    return lax.dot_general(left, right, (((1,), (1,)), ((), ())), preferred_element_type=f32)


def dot_lt(left, right):
    return lax.dot_general(left, right, (((0,), (0,)), ((), ())), preferred_element_type=f32)


def swap_core(values):
    return lax.ppermute(values, "mp", [(i, i ^ 1) for i in range(4)])


def swap_view(values):
    return lax.ppermute(values, "mp", [(i, i ^ 2) for i in range(4)])


def swap_side(values):
    return lax.ppermute(values, "dp", [(i, i ^ 1) for i in range(lax.axis_size("dp"))])


def after(values, *others):
    return lax.optimization_barrier((values, *others))[0]


def run(body, outs, args, us=1.0, scalars=(), scratch=(), hidden=False, left=()):
    return pl.pallas_call(
        body,
        out_shape=[jax.ShapeDtypeStruct(s, d) for s, d in outs],
        in_specs=[
            pl.BlockSpec(
                memory_space=pltpu.SMEM if i in scalars else pl.ANY if i in left else pltpu.VMEM
            )
            for i in range(len(args))
        ],
        out_specs=[pl.BlockSpec(memory_space=pltpu.VMEM) for _ in outs],
        scratch_shapes=list(scratch),
        compiler_params=pltpu.CompilerParams(vmem_limit_bytes=VMEM_LIMIT),
        cost_estimate=pl.CostEstimate(
            flops=int(us * PEAK * (3 if hidden else 0)), bytes_accessed=0, transcendentals=0
        ),
    )(*args)


VMEM_LIMIT = 16 * 1024 * 1024
PEAK = 1.15e9


def norm_parts(values):
    centred = values - jnp.mean(values, axis=-1, keepdims=True)
    rstd = lax.rsqrt(jnp.mean(centred * centred, axis=-1, keepdims=True) + epsilon)
    return centred * rstd, rstd


def join_body(count, *refs):
    base, terms, gain = refs[0], refs[1 : 1 + count], refs[1 + count]
    total = base[...]
    for term in terms:
        total = total + term[...].astype(f32)
    refs[2 + count][...] = total
    refs[3 + count][...] = (norm_parts(total)[0] * gain[...]).astype(bf16)


def join_norm(base, terms, gain):
    outs = [(base.shape, f32), (base.shape, bf16)]
    body = functools.partial(join_body, len(terms))
    return run(body, outs, (base, *terms, gain[None]), us=1.1)


def norm_back_body(count, *refs):
    values, gain, gradient = refs[:3]
    total = refs[3][...].astype(f32)
    for term in refs[4 : 3 + count]:
        total = total + term[...].astype(f32)
    n, rstd = norm_parts(values[...])
    refs[3 + count][...] = jnp.sum(total * n, axis=0, keepdims=True)
    dn = total * gain[...]
    dx = rstd * (
        dn - jnp.mean(dn, axis=-1, keepdims=True) - n * jnp.mean(dn * n, axis=-1, keepdims=True)
    )
    new = gradient[...].astype(f32) + dx
    refs[4 + count][...] = new
    refs[5 + count][...] = new.astype(bf16)


def norm_back(values, gain, gradient, terms):
    outs = [((1, values.shape[1]), f32), (values.shape, f32), (values.shape, bf16)]
    body = functools.partial(norm_back_body, len(terms))
    return run(body, outs, (values, gain[None], gradient, *terms), us=1.5)


def finish_body(sums, qkv, out):
    m = out.shape[1]
    for layer in range(2):
        at = 4 * m * layer
        for i in range(3):
            qkv[layer, i] = sums[:, at + i * m : at + (i + 1) * m].astype(f32)
        out[layer] = sums[:, at + 3 * m : at + 4 * m].astype(f32).T


def ask_body(capacity, target, partner, slot_ref, ask_ref):
    peers = ask_ref.shape[0]
    rows = target.shape[1]
    chosen = lax.broadcasted_iota(i32, (peers, rows), 0) == target[...]
    earlier = lax.broadcasted_iota(i32, (rows, rows), 0) < lax.broadcasted_iota(
        i32, (rows, rows), 1
    )
    before = dot(jnp.where(chosen, 1.0, 0.0).astype(bf16), jnp.where(earlier, 1.0, 0.0).astype(bf16))
    rank = jnp.sum(jnp.where(chosen, before, 0.0), axis=0, keepdims=True).astype(i32)
    slot_ref[...] = target[...] * capacity + rank
    placed = lax.broadcasted_iota(i32, (capacity, rows), 0) == rank
    placed = jnp.where(placed, 1.0, 0.0).astype(bf16)
    high = partner[...] // 32
    low = partner[...] - high * 32
    part = lambda v: dot_rt(jnp.where(chosen, v.astype(f32), 0.0).astype(bf16), placed)
    ask_ref[...] = (part(high) * 32.0 + part(low)).astype(i32)


def one_hot(index, count):
    hit = lax.broadcasted_iota(i32, (count, index.shape[1]), 0) == index[...]
    return jnp.where(hit, 1.0, 0.0).astype(bf16)


def find_body(asked, tokens, found):
    found[...] = dot_lt(one_hot(asked, tokens.shape[0]), tokens[...]).astype(bf16)


def mix_body(slot, replies, own, weight, gain, stream, normed):
    partner = dot_lt(one_hot(slot, replies.shape[0]), replies[...])
    total = weight[...] * own[...].astype(f32) + (1.0 - weight[...]) * partner
    stream[...] = total
    normed[...] = (norm_parts(total)[0] * gain[...]).astype(bf16)


def give_body(slot, weight, gradient, g0, g1, g2, g3, outgoing):
    peers, count, _ = outgoing.shape
    capacity = count - 8
    rows = ((1.0 - weight[...]) * gradient[...]).astype(bf16)
    placed = dot(one_hot(slot, peers * capacity), rows).astype(bf16)
    gains = jnp.concatenate([g0[...], g1[...], g2[...], g3[...]], axis=0)
    high = gains.astype(bf16)
    extra = jnp.concatenate([high.astype(f32), gains - high.astype(f32)], axis=0).astype(bf16)
    for p in range(peers):
        outgoing[p, :capacity, :] = placed[p * capacity : (p + 1) * capacity, :]
        outgoing[p, capacity:, :] = extra


def spread_body(place, asked, returned, gains, *refs):
    near, core, far, far_core, flat = refs
    peers, count, _ = returned.shape
    capacity = count - 8
    rows = near.shape[0]
    total = jnp.zeros((8, near.shape[1]), f32)
    for p in range(peers):
        flat[p * capacity : (p + 1) * capacity, :] = returned[p, :capacity, :]
        total = total + returned[p, capacity:, :].astype(f32)
    gains[...] = total[:4] + total[4:]
    for i, ref in enumerate((near, core, far, far_core)):
        owner = jnp.bitwise_xor(place[0], i)
        ref[...] = dot(one_hot(asked[...] - owner * rows, rows), flat[...])


def gelu_parts(u):
    t = 1.0 / (1.0 + (TAIL_P * 0.5**0.5) * jnp.abs(u))
    poly = TAIL[-1]
    for c in TAIL[-2::-1]:
        poly = poly * t + c
    bell = jnp.exp(-0.5 * u * u)
    tail = 0.5 * poly * t * bell
    phi = jnp.where(u < 0.0, tail, 1.0 - tail)
    return u * phi, phi + u * bell * 0.3989422804014327


def fetch(layer, sources, places, sems):
    copies = [
        pltpu.make_async_copy(source.at[layer], place, sems.at[i])
        for i, (source, place) in enumerate(zip(sources, places))
    ]
    for copy in copies:
        copy.start()
    return copies


def mlp_body(layer, b, up0, up1, down0, down1, mine, theirs, slope, part, up2, down2, sems):
    width = b.shape[1]
    hidden = up0.shape[2]
    rows = b[...]
    copies = fetch(layer, (up1, down1), (up2, down2), sems)
    total = 0.0
    sides = ((mine, up0.at[layer], down0.at[layer]), (theirs, up2, down2))
    for i, (saved, up, down) in enumerate(sides):
        saved[:, :width] = rows
        if i == 1:
            for copy in copies:
                copy.wait()
        for j in range(0, hidden, 256):
            z, dz = gelu_parts(dot(rows, up[:, j : j + 256]))
            saved[:, width + j : width + j + 256] = z.astype(bf16)
            slope[:, i * hidden + j : i * hidden + j + 256] = dz
        total = total + dot(saved[:, width:], down[...])
    part[...] = total.astype(part.dtype)


def fetched(weights):
    shapes = [pltpu.VMEM(w.shape[1:], w.dtype) for w in (weights[1], weights[3])]
    return [*shapes, pltpu.SemaphoreType.DMA((2,))]


def mlp(layer, b, weights, dtype):
    rows, width = b.shape
    hidden = weights[0].shape[2]
    outs = [((rows, width + hidden), bf16)] * 2
    outs += [((rows, 2 * hidden), f32), ((rows, width), dtype)]
    body = functools.partial(mlp_body, layer)
    return run(body, outs, (b, *weights), us=3.5, scratch=fetched(weights), left=(2, 4))


def mlp_back_body(
    layer, g, slope, up0, up1, down0, down1, mine, theirs, part, up2, down2, sems
):
    width = g.shape[1]
    hidden = up0.shape[2]
    rows = g[...]
    copies = fetch(layer, (up1, down1), (up2, down2), sems)
    total = 0.0
    sides = ((mine, up0.at[layer], down0.at[layer]), (theirs, up2, down2))
    for i, (saved, up, down) in enumerate(sides):
        saved[:, :width] = rows
        if i == 1:
            for copy in copies:
                copy.wait()
        for j in range(0, hidden, 256):
            at = i * hidden + j
            dz = dot_rt(rows, down[j : j + 256, :])
            saved[:, width + j : width + j + 256] = (dz * slope[:, at : at + 256]).astype(bf16)
        total = total + dot_rt(saved[:, width:], up[...])
    part[...] = total.astype(part.dtype)


def mlp_back(layer, g, slope, weights, dtype):
    rows, width = g.shape
    hidden = weights[0].shape[2]
    outs = [((rows, width + hidden), bf16)] * 2 + [((rows, width), dtype)]
    body = functools.partial(mlp_back_body, layer)
    return run(body, outs, (g, slope, *weights), us=2.5, scratch=fetched(weights), left=(3, 5))


def mlp_sums_body(*refs):
    ahead, back, sums = refs[:4], refs[4:8], refs[8]
    width = sums.shape[0]
    hidden = sums.shape[1] // 2
    for i, (left, right) in enumerate(((ahead, back), (back, ahead))):
        left = jnp.concatenate([v[:, :width] for v in left], axis=0)
        right = jnp.concatenate([v[:, width:] for v in right], axis=0)
        sums[:, i * hidden : (i + 1) * hidden] = dot_lt(left, right).astype(bf16)


def mlp_sums(width, ahead, back):
    outs = [((width, 2 * (ahead[0].shape[1] - width)), bf16)]
    return run(mlp_sums_body, outs, (*ahead, *back), us=3.5, hidden=True)[0]


def cut_rows(side, values, send, keep, column):
    count, block, _ = send.shape
    n = values.shape[1]
    for z in range(count):
        theirs = pl.multiple_of((2 * z + 1 - side[0]) * block, 8)
        mine = pl.multiple_of((2 * z + side[0]) * block, 8)
        send[z, :, column : column + n] = values[pl.ds(theirs, block), :].astype(bf16)
        keep[z, :, column : column + n] = values[pl.ds(mine, block), :]


def cut_outside(side, peers, grads):
    parts = grads.reshape(peers // 2, 2, -1, grads.shape[1])
    send = lax.dynamic_index_in_dim(parts, 1 - side[0], 1, False)
    return send.astype(bf16), lax.dynamic_index_in_dim(parts, side[0], 1, False)


def groups_of(n):
    return [(j, min(128, n - j)) for j in range(0, n, 128)]


def places(width, n):
    stride = -(-n // 128) * 128
    return [width + i * stride for i in range(5)]


def view_bias(rows, place, counts, other):
    half = lax.rem(place[0], 2)
    count = counts[0, jnp.bitwise_xor(lax.div(place[0], 2), other)]
    index = lax.broadcasted_iota(i32, (2 * rows, 1), 0)
    position = jnp.where(index < rows, index + half * rows, index - half * rows)
    return jnp.where(position < count, 0.0, masked_score).astype(f32)


def masked(values, head):
    if values.shape[1] == HD:
        return values
    keep = lax.broadcasted_iota(i32, values.shape, 1) // HD == head
    return jnp.where(keep, values, jnp.zeros_like(values))


def attend_core(from_q, from_k, lse, bias, width, n):
    q0, k0, v0, o0, _ = places(width, n)
    lse[...] = jnp.zeros(lse.shape, f32)
    for j, w in groups_of(n):
        q = from_q[:, q0 + j : q0 + j + w] * jnp.asarray(SCALE, bf16)
        k = from_k[:, k0 + j : k0 + j + w]
        v = from_k[:, v0 + j : v0 + j + w]
        out = jnp.zeros((w, q.shape[0]), f32)
        for head in range(w // HD):
            s = dot_rt(k, masked(q, head)) + bias
            top = jnp.max(s, axis=0, keepdims=True)
            e = jnp.exp(s - top)
            total = jnp.sum(e, axis=0, keepdims=True)
            weights = (e * (1.0 / total)).astype(bf16)
            at = j // HD + head
            lse[at : at + 1, :] = top + jnp.log(total)
            out = out + dot_lt(masked(v, head), weights)
        from_q[:, o0 + j : o0 + j + w] = out.T.astype(bf16)


def attend_back_core(from_q, from_k, do, lse, bias, back, width, n):
    q0, k0, v0, _, _ = places(width, n)
    for j, w in groups_of(n):
        q = from_q[:, q0 + j : q0 + j + w] * jnp.asarray(SCALE, bf16)
        k = from_k[:, k0 + j : k0 + j + w]
        v = from_k[:, v0 + j : v0 + j + w]
        d = do[:, j : j + w]
        dv = jnp.zeros(q.shape, f32)
        dk = jnp.zeros(q.shape, f32)
        dq = jnp.zeros((w, q.shape[0]), f32)
        for head in range(w // HD):
            qm, dm, km = masked(q, head), masked(d, head), masked(k, head)
            at = j // HD + head
            p = jnp.exp(dot_rt(k, qm) + bias - lse[at : at + 1, :])
            dp = dot_rt(v, dm)
            centre = jnp.sum(p * dp, axis=0, keepdims=True)
            ds = (p * (dp - centre)).astype(bf16)
            dv = dv + dot(p.astype(bf16), dm)
            dk = dk + dot(ds, qm)
            dq = dq + dot_lt(km, ds)
        back[:, q0 + j : q0 + j + w] = (dq.T * SCALE).astype(bf16)
        back[:, k0 + j : k0 + j + w] = dk.astype(bf16)
        back[:, v0 + j : v0 + j + w] = dv.astype(bf16)


def join_weights(own, far, own_o, far_o, w, wo):
    m = own_o.shape[1]
    for i in range(3):
        w[2 * i * m : (2 * i + 1) * m, :] = own[0, i]
        w[(2 * i + 1) * m : (2 * i + 2) * m, :] = far[0, i]
    wo[:m, :] = own_o[0]
    wo[m:, :] = far_o[0]


def attend_body(place, counts, a0, a1, own, far, own_o, far_o, saved, lse, p0, p1, w, wo):
    join_weights(own, far, own_o, far_o, w, wo)
    rows, width = p0.shape
    n = wo.shape[0]
    q0, _, _, o0, _ = places(width, n)
    a = jnp.concatenate([a0[...], a1[...]], axis=0)
    saved[:, :width] = a
    saved[:, q0:o0] = dot_rt(a, w[...]).astype(bf16)
    attend_core(saved, saved, lse, view_bias(rows, place, counts, 0), width, n)
    p0[...] = dot(saved[:rows, o0:], wo[...])
    p1[...] = dot(saved[rows:, o0:], wo[...])


def attend(place, counts, shares, weights):
    rows, width = shares[0].shape
    n = 2 * weights[2].shape[1]
    outs = [((2 * rows, width + 4 * n), bf16), ((8, 2 * rows), f32)]
    outs += [((rows, width), f32)] * 2
    scratch = [pltpu.VMEM((3 * n, width), bf16), pltpu.VMEM((n, width), bf16)]
    return run(
        attend_body,
        outs,
        (place, counts, *shares, *weights),
        us=6.5,
        scalars=(0, 1),
        scratch=scratch,
    )


def attend_back_body(
    place, counts, g0, g1, saved, lse, own, far, own_o, far_o, back, p0, p1, do, w, wo
):
    join_weights(own, far, own_o, far_o, w, wo)
    rows, width = g0.shape
    n = wo.shape[0]
    g = jnp.concatenate([g0[...], g1[...]], axis=0)
    back[:, :width] = g
    do[...] = dot_rt(g, wo[...]).astype(bf16)
    bias = view_bias(rows, place, counts, 0)
    attend_back_core(saved, saved, do, lse, bias, back, width, n)
    p0[...] = dot(back[:rows, width:], w[...])
    p1[...] = dot(back[rows:, width:], w[...])


def attend_back(place, counts, g, saved, lse, weights):
    rows, width = g[0].shape
    n = 2 * weights[2].shape[1]
    return run(
        attend_back_body,
        [((2 * rows, width + 3 * n), bf16)] + [((rows, width), f32)] * 2,
        (place, counts, *g, saved, lse, *weights),
        us=8.0,
        scalars=(0, 1),
        scratch=[
            pltpu.VMEM((2 * rows, n), bf16),
            pltpu.VMEM((3 * n, width), bf16),
            pltpu.VMEM((n, width), bf16),
        ],
    )


def attend_sums_body(cut, side, saved, back, near, far, *refs):
    total = refs[-1]
    width, n = near.shape
    m = n // 2
    q0, k0, v0, o0, _ = places(width, n)
    a = saved[:, :width]
    for i in range(2):
        part = dot_lt(a, back[:, q0 + i * n : q0 + (i + 1) * n])
        near[:, i * m : (i + 1) * m] = part[:, :m]
        far[:, i * m : (i + 1) * m] = part[:, m:].astype(bf16)
    for i in range(2):
        if i == 0:
            part = dot_lt(a, back[:, v0 : v0 + n])
        else:
            part = dot_lt(back[:, :width], saved[:, o0 : o0 + n])
        total[:, i * m : (i + 1) * m] = part[:, :m]
        total[:, n + i * m : n + (i + 1) * m] = part[:, m:]
    if cut:
        cut_rows(side, total, refs[0], refs[1], 0)


def attend_sums(side, peers, width, saved, back):
    n = (saved.shape[1] - width) // 4
    block = width // peers
    cut = block % 16 == 0
    outs = [((width, n), f32), ((width, n), bf16)]
    scratch = []
    if cut:
        outs += [((peers // 2, block, 2 * n), bf16), ((peers // 2, block, 2 * n), f32)]
        scratch = [pltpu.VMEM((width, 2 * n), f32)]
    else:
        outs += [((width, 2 * n), f32)]
    out = run(
        functools.partial(attend_sums_body, cut),
        outs,
        (side, saved, back),
        us=3.0,
        scalars=(0,),
        scratch=scratch,
    )
    return out if cut else (*out[:2], *cut_outside(side, peers, out[2]))


def cross_body(
    place, counts, a0, a1, a2, a3, w, wo, own, far, lse, lse_far, p0, p1, p2, p3
):
    rows, width = p0.shape
    n = wo.shape[1]
    q0, k0, v0, o0, _ = places(width, n)
    for saved, halves in ((own, (a0, a1)), (far, (a2, a3))):
        a = jnp.concatenate([halves[0][...], halves[1][...]], axis=0)
        saved[:, :width] = a
        for i, at in enumerate((q0, k0, v0)):
            saved[:, at : at + n] = dot_rt(a, w[1, i]).astype(bf16)
    attend_core(far, own, lse_far, view_bias(rows, place, counts, 0), width, n)
    p2[...] = dot(far[:rows, o0 : o0 + n], wo[1])
    p3[...] = dot(far[rows:, o0 : o0 + n], wo[1])
    attend_core(own, far, lse, view_bias(rows, place, counts, 1), width, n)
    p0[...] = dot(own[:rows, o0 : o0 + n], wo[1])
    p1[...] = dot(own[rows:, o0 : o0 + n], wo[1])


def cross(place, counts, shares, w, wo):
    rows, width = shares[0].shape
    wide = places(width, wo.shape[1])[4]
    outs = [((2 * rows, wide), bf16)] * 2 + [((8, 2 * rows), f32)] * 2
    outs += [((rows, width), f32)] * 4
    args = (place, counts, *shares, w, wo)
    return run(cross_body, outs, args, us=6.5, scalars=(0, 1))


def cross_back_body(other, place, counts, g0, g1, from_q, from_k, lse, wo, back, do):
    rows, width = g0.shape
    n = wo.shape[1]
    g = jnp.concatenate([g0[...], g1[...]], axis=0)
    back[:, :width] = g
    do[...] = dot_rt(g, wo[1]).astype(bf16)
    bias = view_bias(rows, place, counts, other)
    attend_back_core(from_q, from_k, do, lse, bias, back, width, n)


def cross_back(other, place, counts, g, from_q, from_k, lse, wo):
    rows, width = g[0].shape
    n = wo.shape[1]
    return run(
        functools.partial(cross_back_body, other),
        [((2 * rows, places(width, n)[3]), bf16)],
        (place, counts, *g, from_q, from_k, lse, wo),
        us=4.0,
        scalars=(0, 1),
        scratch=[pltpu.VMEM((2 * rows, n), bf16)],
    )[0]


def cross_rows_body(own, far, w, p0, p1, p2, p3):
    rows, width = p0.shape
    n = w.shape[2]
    q0, k0, v0, _, _ = places(width, n)
    for queries, keys, parts in ((far, own, (p2, p3)), (own, far, (p0, p1))):
        for i, part in enumerate(parts):
            at = slice(i * rows, (i + 1) * rows)
            part[...] = (
                dot(queries[at, q0 : q0 + n], w[1, 0])
                + dot(keys[at, k0 : k0 + n], w[1, 1])
                + dot(keys[at, v0 : v0 + n], w[1, 2])
            )


def cross_rows(rows, width, own, far, w):
    return run(cross_rows_body, [((rows, width), f32)] * 4, (own, far, w), us=2.0)


def cross_sums_body(own, far, own_back, far_back, sums):
    width = sums.shape[0]
    n = sums.shape[1] // 4
    q0, k0, v0, o0, _ = places(width, n)
    rows = lambda first, second, at, size: jnp.concatenate(
        [first[:, at : at + size], second[:, at : at + size]], axis=0
    )
    queries = rows(own, far, 0, width)
    keys = rows(far, own, 0, width)
    parts = [
        (queries, rows(own_back, far_back, q0, n)),
        (keys, rows(own_back, far_back, k0, n)),
        (keys, rows(own_back, far_back, v0, n)),
        (rows(own_back, far_back, 0, width), rows(own, far, o0, n)),
    ]
    for i, (left, right) in enumerate(parts):
        sums[:, i * n : (i + 1) * n] = dot_lt(left, right).astype(bf16)


def cross_sums(width, n, own, far, own_back, far_back):
    return run(
        cross_sums_body, [((width, 4 * n), bf16)], (own, far, own_back, far_back), us=3.0
    )[0]


def on_device(
    tokens,
    cotangent,
    mix_coef,
    partner_dev,
    partner_row,
    view_counts,
    w_qkv,
    w_out,
    w_up,
    w_down,
    gain_attn,
    gain_mlp,
):
    peers = lax.axis_size("dp")
    rows = mix_coef.shape[0]
    width = tokens.shape[1]
    mine = w_qkv.shape[-1]
    block = width // peers
    capacity = max(2, 2 * rows // peers)
    slots = peers * capacity
    place = lax.axis_index("mp").astype(i32)[None]
    side = (lax.axis_index("dp") % 2).astype(i32)[None]
    weight_own = mix_coef[:, None]

    slot, requests = run(
        functools.partial(ask_body, capacity),
        [((1, rows), i32), ((peers, capacity), i32)],
        (partner_dev.reshape(1, rows), partner_row.reshape(1, rows)),
    )

    own_w = w_qkv.transpose(0, 2, 3, 1)
    far_o = swap_view(w_out[:1])
    far_w = swap_view(own_w[:1])
    asked = lax.all_to_all(requests, "dp", split_axis=0, concat_axis=0, tiled=True)
    asked = after(asked, far_o).reshape(1, slots)
    (found,) = run(find_body, [((slots, width), bf16)], (asked, tokens), us=2.0)
    replies = lax.all_to_all(
        found.reshape(peers, capacity, width), "dp", split_axis=0, concat_axis=0, tiled=True
    )
    own_tokens = lax.dynamic_slice_in_dim(tokens, place[0] * rows, rows, 0)
    replies, far_w, own_tokens = lax.optimization_barrier((replies, far_w, own_tokens))
    stream, a_share = run(
        mix_body,
        [((rows, width), f32), ((rows, width), bf16)],
        (slot, replies.reshape(slots, width), own_tokens, weight_own, gain_attn[:1]),
        us=1.5,
    )
    mlp_w = (w_up, swap_core(w_up), w_down, swap_core(w_down))

    def feed_forward(layer, b_share):
        b_far = swap_view(b_share)
        own, own_core, slope_own, part = mlp(layer, b_share, mlp_w, f32)
        far, far_core, slope_far, there = mlp(layer, after(b_far, part), mlp_w, bf16)
        kept = (own, swap_core(own_core), far, swap_core(far_core))
        return kept, (slope_own, slope_far), (part, swap_view(there))

    def feed_forward_back(layer, g_share, kept, slope, due=()):
        g_far = swap_view(g_share)
        own, own_core, part = mlp_back(layer, g_share, slope[0], mlp_w, f32)
        g_far = after(g_far, part)
        far, far_core, there = mlp_back(layer, g_far, slope[1], mlp_w, bf16)
        arrived = swap_view(there)
        back = (own, swap_core(own_core), far, swap_core(far_core))
        sums = mlp_sums(width, kept, after(back, *due))
        return sums, (part, after(arrived, sums))

    first_in = stream
    weights = (own_w[:1], far_w, w_out[:1], far_o)
    kept0, lse0, part, part_core = attend(place, view_counts, (a_share, swap_core(a_share)), weights)
    first_mid, b_share = join_norm(first_in, (part, swap_core(part_core)), gain_mlp[0])
    mlp0, slope0, terms = feed_forward(0, b_share)

    second_in, a_share = join_norm(first_mid, terms, gain_attn[1])
    a_far = swap_view(a_share)
    shares = (a_share, swap_core(a_share), a_far, swap_core(a_far))
    own1, far1, lse1, lse1_far, part, part_core, there, there_core = cross(
        place, view_counts, shares, own_w, w_out
    )
    arrived = swap_view((there + swap_core(there_core)).astype(bf16))
    second_mid, b_share = join_norm(second_in, (part, swap_core(part_core), arrived), gain_mlp[1])
    mlp1, slope1, terms = feed_forward(1, b_share)
    layer_output = (second_mid + terms[0] + terms[1].astype(f32)).astype(bf16)

    def along_z(values):
        groups = [list(range(s, peers, 2)) for s in range(2)]
        return lax.psum_scatter(
            values, "dp", scatter_dimension=0, tiled=True, axis_index_groups=groups
        )

    def between_sides(values):
        send = lax.dynamic_slice_in_dim(values, (1 - side[0]) * block, block, 0)
        keep = lax.dynamic_slice_in_dim(values, side[0] * block, block, 0)
        return keep.astype(f32) + swap_side(send).astype(f32)

    gain_parts = [None] * 4
    mlp_sum1, terms = feed_forward_back(1, cotangent, mlp1, slope1)
    sum_mlp1 = along_z(mlp_sum1)
    gain_parts[3], gradient, g_share = norm_back(second_mid, gain_mlp[1], cotangent, terms)

    g_far = swap_view(g_share)
    own_back = cross_back(
        1, place, view_counts, (g_share, swap_core(g_share)), own1, far1, lse1, w_out
    )
    g_far = after(g_far, own_back)
    far_back = cross_back(
        0, place, view_counts, (g_far, swap_core(g_far)), far1, own1, lse1_far, w_out
    )
    part, part_core, there, there_core = cross_rows(rows, width, own_back, far_back, own_w)
    arrived = swap_view((there + swap_core(there_core)).astype(bf16))
    attn_sum1 = cross_sums(width, mine, own1, far1, own_back, far_back)
    terms = (part, swap_core(part_core), after(arrived, attn_sum1))
    attn_cut = cut_outside(side, peers, attn_sum1)
    got_attn1 = swap_side(attn_cut[0])
    gain_parts[1], gradient, g_share = norm_back(second_in, gain_attn[1], gradient, terms)

    mlp_sum0, terms = feed_forward_back(0, g_share, mlp0, slope0)
    sum_mlp0 = along_z(after(mlp_sum0, sum_mlp1))
    gain_parts[2], gradient, g_share = norm_back(first_mid, gain_mlp[0], gradient, terms)

    back, part, part_core = attend_back(
        place, view_counts, (g_share, swap_core(g_share)), kept0, lse0, weights
    )
    back, got_attn1 = lax.optimization_barrier((back, got_attn1))
    near, far, send, keep = attend_sums(side, peers, width, kept0, back)
    gain_parts[0], gradient, _ = norm_back(
        first_in, gain_attn[0], gradient, (part, swap_core(part_core))
    )

    (outgoing,) = run(
        give_body,
        [((peers, capacity + 8, width), bf16)],
        (slot, weight_own, gradient, *gain_parts),
        us=1.5,
    )
    returned = lax.all_to_all(outgoing, "dp", split_axis=0, concat_axis=0, tiled=True)

    got_far, got_send, _ = lax.optimization_barrier((swap_view(far), swap_side(send), outgoing))
    send_qk, keep_qk = cut_outside(side, peers, near + got_far.astype(f32))
    keep_vo = keep + got_send.astype(f32)
    n = near.shape[1]
    sum_qk = (keep_qk + swap_side(send_qk).astype(f32)).astype(bf16)
    sum_vo = (keep_vo[:, :, :n] + swap_view(keep_vo[:, :, n:].astype(bf16)).astype(f32)).astype(bf16)
    first_sum = (attn_cut[1].astype(f32) + got_attn1.astype(f32)).astype(bf16)
    joined = jnp.concatenate([sum_qk, sum_vo, first_sum], axis=2)
    joined = joined.reshape(peers // 2 * block, 8 * mine)
    joined, sum_mlp0, returned = lax.optimization_barrier((joined, sum_mlp0, returned))
    attn_sum = along_z(joined)
    mlp_all = jnp.stack([between_sides(sum_mlp0), between_sides(sum_mlp1)])
    gain_sum, part, part_core, there, there_core = run(
        spread_body,
        [((4, width), f32)] + [((rows, width), f32)] * 4,
        (place, asked, returned),
        us=1.5,
        scalars=(0,),
        scratch=[pltpu.VMEM((slots, width), bf16)],
    )
    gain_sum = gain_sum + swap_core(gain_sum)
    gain_sum = gain_sum + swap_view(gain_sum)
    gain_sum = lax.dynamic_slice_in_dim(gain_sum, lax.axis_index("dp") * block, block, 1)
    arrived = swap_view((there + swap_core(there_core)).astype(bf16))
    grad_tokens = weight_own * gradient + part + swap_core(part_core) + arrived.astype(f32)

    grad_qkv, grad_out = run(
        finish_body, [((2, 3, block, mine), f32), ((2, mine, block), f32)], (attn_sum,)
    )
    hidden = mlp_all.shape[-1] // 2
    return (
        layer_output,
        grad_tokens,
        grad_qkv.transpose(0, 2, 1, 3),
        grad_out,
        mlp_all[:, :, :hidden],
        mlp_all[:, :, hidden:].transpose(0, 2, 1),
        gain_sum[:2],
        gain_sum[2:],
    )


def solution(mesh):
    placed = (
        P("dp", None),
        P(("dp", "mp"), None),
        P(("dp", "mp")),
        P(("dp", "mp"), None),
        P(("dp", "mp")),
        P("dp", None),
        P(None, None, None, "mp"),
        P(None, "mp", None),
        P(None, None, "mp"),
        P(None, "mp", None),
        P(),
        P(),
    )
    return jax.shard_map(
        on_device,
        mesh=mesh,
        in_specs=placed,
        out_specs=(
            P(("dp", "mp"), None),
            P(("dp", "mp"), None),
            P(None, "dp", None, "mp"),
            P(None, "mp", "dp"),
            P(None, "dp", "mp"),
            P(None, "mp", "dp"),
            P(None, "dp"),
            P(None, "dp"),
        ),
        check_vma=False,
    )
```

```python
import functools

import jax
import jax.numpy as jnp
from jax import lax
from jax.experimental import pallas as pl
from jax.experimental.pallas import tpu as pltpu
from jax.sharding import PartitionSpec as P

HD = 64
SCALE = HD ** (-0.5)
epsilon = 1e-06
masked_score = -1000000000.0
bf16 = jnp.bfloat16
f32 = jnp.float32
i32 = jnp.int32

TAIL_P = 0.38
TAIL = (
    0.2144098248509563,
    0.21394460416600933,
    0.20368405029440034,
    0.13968567743708352,
    0.2272053511927878,
    -0.15681775904774625,
    0.3593185352386043,
    -0.25984971762641107,
    0.058419421394547984,
)


def dot(left, right):
    return jnp.dot(left, right, preferred_element_type=f32)


def dot_rt(left, right):
    return lax.dot_general(left, right, (((1,), (1,)), ((), ())), preferred_element_type=f32)


def dot_lt(left, right):
    return lax.dot_general(left, right, (((0,), (0,)), ((), ())), preferred_element_type=f32)


def swap_core(values):
    return lax.ppermute(values, "mp", [(i, i ^ 1) for i in range(4)])


def swap_view(values):
    return lax.ppermute(values, "mp", [(i, i ^ 2) for i in range(4)])


def swap_side(values):
    return lax.ppermute(values, "dp", [(i, i ^ 1) for i in range(lax.axis_size("dp"))])


def after(values, *others):
    return lax.optimization_barrier((values, *others))[0]


def run(body, outs, args, us=1.0, scalars=(), scratch=(), hidden=False, left=()):
    return pl.pallas_call(
        body,
        out_shape=[jax.ShapeDtypeStruct(s, d) for s, d in outs],
        in_specs=[
            pl.BlockSpec(
                memory_space=pltpu.SMEM if i in scalars else pl.ANY if i in left else pltpu.VMEM
            )
            for i in range(len(args))
        ],
        out_specs=[pl.BlockSpec(memory_space=pltpu.VMEM) for _ in outs],
        scratch_shapes=list(scratch),
        compiler_params=pltpu.CompilerParams(vmem_limit_bytes=VMEM_LIMIT),
        cost_estimate=pl.CostEstimate(
            flops=int(us * PEAK * (3 if hidden else 1)), bytes_accessed=0, transcendentals=0
        ),
    )(*args)


VMEM_LIMIT = 16 * 1024 * 1024
PEAK = 1.15e9


def norm_parts(values):
    centred = values - jnp.mean(values, axis=-1, keepdims=True)
    rstd = lax.rsqrt(jnp.mean(centred * centred, axis=-1, keepdims=True) + epsilon)
    return centred * rstd, rstd


def join_body(count, *refs):
    base, terms, gain = refs[0], refs[1 : 1 + count], refs[1 + count]
    total = base[...]
    for term in terms:
        total = total + term[...].astype(f32)
    refs[2 + count][...] = total
    refs[3 + count][...] = (norm_parts(total)[0] * gain[...]).astype(bf16)


def join_norm(base, terms, gain):
    outs = [(base.shape, f32), (base.shape, bf16)]
    body = functools.partial(join_body, len(terms))
    return run(body, outs, (base, *terms, gain[None]), us=1.1)


def norm_back_body(count, *refs):
    values, gain, gradient = refs[:3]
    total = refs[3][...].astype(f32)
    for term in refs[4 : 3 + count]:
        total = total + term[...].astype(f32)
    n, rstd = norm_parts(values[...])
    refs[3 + count][...] = jnp.sum(total * n, axis=0, keepdims=True)
    dn = total * gain[...]
    dx = rstd * (
        dn - jnp.mean(dn, axis=-1, keepdims=True) - n * jnp.mean(dn * n, axis=-1, keepdims=True)
    )
    new = gradient[...].astype(f32) + dx
    refs[4 + count][...] = new
    refs[5 + count][...] = new.astype(bf16)


def norm_back(values, gain, gradient, terms):
    outs = [((1, values.shape[1]), f32), (values.shape, f32), (values.shape, bf16)]
    body = functools.partial(norm_back_body, len(terms))
    return run(body, outs, (values, gain[None], gradient, *terms), us=1.5)


def finish_body(sums, qkv, out):
    m = out.shape[1]
    for layer in range(2):
        at = 4 * m * layer
        for i in range(3):
            qkv[layer, i] = sums[:, at + i * m : at + (i + 1) * m].astype(f32)
        out[layer] = sums[:, at + 3 * m : at + 4 * m].astype(f32).T


def ask_body(capacity, target, partner, slot_ref, ask_ref):
    peers = ask_ref.shape[0]
    rows = target.shape[1]
    chosen = lax.broadcasted_iota(i32, (peers, rows), 0) == target[...]
    earlier = lax.broadcasted_iota(i32, (rows, rows), 0) < lax.broadcasted_iota(
        i32, (rows, rows), 1
    )
    before = dot(jnp.where(chosen, 1.0, 0.0).astype(bf16), jnp.where(earlier, 1.0, 0.0).astype(bf16))
    rank = jnp.sum(jnp.where(chosen, before, 0.0), axis=0, keepdims=True).astype(i32)
    slot_ref[...] = target[...] * capacity + rank
    placed = lax.broadcasted_iota(i32, (capacity, rows), 0) == rank
    placed = jnp.where(placed, 1.0, 0.0).astype(bf16)
    high = partner[...] // 32
    low = partner[...] - high * 32
    part = lambda v: dot_rt(jnp.where(chosen, v.astype(f32), 0.0).astype(bf16), placed)
    ask_ref[...] = (part(high) * 32.0 + part(low)).astype(i32)


def one_hot(index, count):
    hit = lax.broadcasted_iota(i32, (count, index.shape[1]), 0) == index[...]
    return jnp.where(hit, 1.0, 0.0).astype(bf16)


def find_body(asked, tokens, found):
    found[...] = dot_lt(one_hot(asked, tokens.shape[0]), tokens[...]).astype(bf16)


def mix_body(slot, replies, own, weight, gain, stream, normed):
    partner = dot_lt(one_hot(slot, replies.shape[0]), replies[...])
    total = weight[...] * own[...].astype(f32) + (1.0 - weight[...]) * partner
    stream[...] = total
    normed[...] = (norm_parts(total)[0] * gain[...]).astype(bf16)


def give_body(slot, weight, gradient, g0, g1, g2, g3, outgoing):
    peers, count, _ = outgoing.shape
    capacity = count - 8
    rows = ((1.0 - weight[...]) * gradient[...]).astype(bf16)
    placed = dot(one_hot(slot, peers * capacity), rows).astype(bf16)
    gains = jnp.concatenate([g0[...], g1[...], g2[...], g3[...]], axis=0)
    high = gains.astype(bf16)
    extra = jnp.concatenate([high.astype(f32), gains - high.astype(f32)], axis=0).astype(bf16)
    for p in range(peers):
        outgoing[p, :capacity, :] = placed[p * capacity : (p + 1) * capacity, :]
        outgoing[p, capacity:, :] = extra


def spread_body(place, asked, returned, gains, *refs):
    near, core, far, far_core, flat = refs
    peers, count, _ = returned.shape
    capacity = count - 8
    rows = near.shape[0]
    total = jnp.zeros((8, near.shape[1]), f32)
    for p in range(peers):
        flat[p * capacity : (p + 1) * capacity, :] = returned[p, :capacity, :]
        total = total + returned[p, capacity:, :].astype(f32)
    gains[...] = total[:4] + total[4:]
    for i, ref in enumerate((near, core, far, far_core)):
        owner = jnp.bitwise_xor(place[0], i)
        ref[...] = dot(one_hot(asked[...] - owner * rows, rows), flat[...])


def gelu_parts(u):
    t = 1.0 / (1.0 + (TAIL_P * 0.5**0.5) * jnp.abs(u))
    poly = TAIL[-1]
    for c in TAIL[-2::-1]:
        poly = poly * t + c
    bell = jnp.exp(-0.5 * u * u)
    tail = 0.5 * poly * t * bell
    phi = jnp.where(u < 0.0, tail, 1.0 - tail)
    return u * phi, phi + u * bell * 0.3989422804014327


def fetch(layer, sources, places, sems):
    copies = [
        pltpu.make_async_copy(source.at[layer], place, sems.at[i])
        for i, (source, place) in enumerate(zip(sources, places))
    ]
    for copy in copies:
        copy.start()
    return copies


def mlp_body(layer, b, up0, up1, down0, down1, mine, theirs, slope, part, up2, down2, sems):
    width = b.shape[1]
    hidden = up0.shape[2]
    rows = b[...]
    copies = fetch(layer, (up1, down1), (up2, down2), sems)
    total = 0.0
    sides = ((mine, up0.at[layer], down0.at[layer]), (theirs, up2, down2))
    for i, (saved, up, down) in enumerate(sides):
        saved[:, :width] = rows
        if i == 1:
            for copy in copies:
                copy.wait()
        for j in range(0, hidden, 256):
            z, dz = gelu_parts(dot(rows, up[:, j : j + 256]))
            saved[:, width + j : width + j + 256] = z.astype(bf16)
            slope[:, i * hidden + j : i * hidden + j + 256] = dz
        total = total + dot(saved[:, width:], down[...])
    part[...] = total.astype(part.dtype)


def fetched(weights):
    shapes = [pltpu.VMEM(w.shape[1:], w.dtype) for w in (weights[1], weights[3])]
    return [*shapes, pltpu.SemaphoreType.DMA((2,))]


def mlp(layer, b, weights, dtype):
    rows, width = b.shape
    hidden = weights[0].shape[2]
    outs = [((rows, width + hidden), bf16)] * 2
    outs += [((rows, 2 * hidden), f32), ((rows, width), dtype)]
    body = functools.partial(mlp_body, layer)
    return run(body, outs, (b, *weights), us=3.5, scratch=fetched(weights), left=(2, 4))


def mlp_back_body(
    layer, g, slope, up0, up1, down0, down1, mine, theirs, part, up2, down2, sems
):
    width = g.shape[1]
    hidden = up0.shape[2]
    rows = g[...]
    copies = fetch(layer, (up1, down1), (up2, down2), sems)
    total = 0.0
    sides = ((mine, up0.at[layer], down0.at[layer]), (theirs, up2, down2))
    for i, (saved, up, down) in enumerate(sides):
        saved[:, :width] = rows
        if i == 1:
            for copy in copies:
                copy.wait()
        for j in range(0, hidden, 256):
            at = i * hidden + j
            dz = dot_rt(rows, down[j : j + 256, :])
            saved[:, width + j : width + j + 256] = (dz * slope[:, at : at + 256]).astype(bf16)
        total = total + dot_rt(saved[:, width:], up[...])
    part[...] = total.astype(part.dtype)


def mlp_back(layer, g, slope, weights, dtype):
    rows, width = g.shape
    hidden = weights[0].shape[2]
    outs = [((rows, width + hidden), bf16)] * 2 + [((rows, width), dtype)]
    body = functools.partial(mlp_back_body, layer)
    return run(body, outs, (g, slope, *weights), us=2.5, scratch=fetched(weights), left=(3, 5))


def mlp_sums_body(*refs):
    ahead, back, sums = refs[:4], refs[4:8], refs[8]
    width = sums.shape[0]
    hidden = sums.shape[1] // 2
    for i, (left, right) in enumerate(((ahead, back), (back, ahead))):
        left = jnp.concatenate([v[:, :width] for v in left], axis=0)
        right = jnp.concatenate([v[:, width:] for v in right], axis=0)
        sums[:, i * hidden : (i + 1) * hidden] = dot_lt(left, right).astype(bf16)


def mlp_sums(width, ahead, back):
    outs = [((width, 2 * (ahead[0].shape[1] - width)), bf16)]
    return run(mlp_sums_body, outs, (*ahead, *back), us=3.5, hidden=True)[0]


def cut_rows(side, values, send, keep, column):
    count, block, _ = send.shape
    n = values.shape[1]
    for z in range(count):
        theirs = pl.multiple_of((2 * z + 1 - side[0]) * block, 8)
        mine = pl.multiple_of((2 * z + side[0]) * block, 8)
        send[z, :, column : column + n] = values[pl.ds(theirs, block), :].astype(bf16)
        keep[z, :, column : column + n] = values[pl.ds(mine, block), :]


def cut_outside(side, peers, grads):
    parts = grads.reshape(peers // 2, 2, -1, grads.shape[1])
    send = lax.dynamic_index_in_dim(parts, 1 - side[0], 1, False)
    return send.astype(bf16), lax.dynamic_index_in_dim(parts, side[0], 1, False)


def groups_of(n):
    return [(j, min(128, n - j)) for j in range(0, n, 128)]


def places(width, n):
    stride = -(-n // 128) * 128
    return [width + i * stride for i in range(5)]


def view_bias(rows, place, counts, other):
    half = lax.rem(place[0], 2)
    count = counts[0, jnp.bitwise_xor(lax.div(place[0], 2), other)]
    index = lax.broadcasted_iota(i32, (2 * rows, 1), 0)
    position = jnp.where(index < rows, index + half * rows, index - half * rows)
    return jnp.where(position < count, 0.0, masked_score).astype(f32)


def masked(values, head):
    if values.shape[1] == HD:
        return values
    keep = lax.broadcasted_iota(i32, values.shape, 1) // HD == head
    return jnp.where(keep, values, jnp.zeros_like(values))


def attend_core(from_q, from_k, lse, bias, width, n):
    q0, k0, v0, o0, _ = places(width, n)
    lse[...] = jnp.zeros(lse.shape, f32)
    for j, w in groups_of(n):
        q = from_q[:, q0 + j : q0 + j + w] * jnp.asarray(SCALE, bf16)
        k = from_k[:, k0 + j : k0 + j + w]
        v = from_k[:, v0 + j : v0 + j + w]
        out = jnp.zeros((w, q.shape[0]), f32)
        for head in range(w // HD):
            s = dot_rt(k, masked(q, head)) + bias
            top = jnp.max(s, axis=0, keepdims=True)
            e = jnp.exp(s - top)
            total = jnp.sum(e, axis=0, keepdims=True)
            weights = (e * (1.0 / total)).astype(bf16)
            at = j // HD + head
            lse[at : at + 1, :] = top + jnp.log(total)
            out = out + dot_lt(masked(v, head), weights)
        from_q[:, o0 + j : o0 + j + w] = out.T.astype(bf16)


def attend_back_core(from_q, from_k, do, lse, bias, back, width, n):
    q0, k0, v0, _, _ = places(width, n)
    for j, w in groups_of(n):
        q = from_q[:, q0 + j : q0 + j + w] * jnp.asarray(SCALE, bf16)
        k = from_k[:, k0 + j : k0 + j + w]
        v = from_k[:, v0 + j : v0 + j + w]
        d = do[:, j : j + w]
        dv = jnp.zeros(q.shape, f32)
        dk = jnp.zeros(q.shape, f32)
        dq = jnp.zeros((w, q.shape[0]), f32)
        for head in range(w // HD):
            qm, dm, km = masked(q, head), masked(d, head), masked(k, head)
            at = j // HD + head
            p = jnp.exp(dot_rt(k, qm) + bias - lse[at : at + 1, :])
            dp = dot_rt(v, dm)
            centre = jnp.sum(p * dp, axis=0, keepdims=True)
            ds = (p * (dp - centre)).astype(bf16)
            dv = dv + dot(p.astype(bf16), dm)
            dk = dk + dot(ds, qm)
            dq = dq + dot_lt(km, ds)
        back[:, q0 + j : q0 + j + w] = (dq.T * SCALE).astype(bf16)
        back[:, k0 + j : k0 + j + w] = dk.astype(bf16)
        back[:, v0 + j : v0 + j + w] = dv.astype(bf16)


def join_weights(own, far, own_o, far_o, w, wo):
    m = own_o.shape[1]
    for i in range(3):
        w[2 * i * m : (2 * i + 1) * m, :] = own[0, i]
        w[(2 * i + 1) * m : (2 * i + 2) * m, :] = far[0, i]
    wo[:m, :] = own_o[0]
    wo[m:, :] = far_o[0]


def attend_body(place, counts, a0, a1, own, far, own_o, far_o, saved, lse, p0, p1, w, wo):
    join_weights(own, far, own_o, far_o, w, wo)
    rows, width = p0.shape
    n = wo.shape[0]
    q0, _, _, o0, _ = places(width, n)
    a = jnp.concatenate([a0[...], a1[...]], axis=0)
    saved[:, :width] = a
    saved[:, q0:o0] = dot_rt(a, w[...]).astype(bf16)
    attend_core(saved, saved, lse, view_bias(rows, place, counts, 0), width, n)
    p0[...] = dot(saved[:rows, o0:], wo[...])
    p1[...] = dot(saved[rows:, o0:], wo[...])


def attend(place, counts, shares, weights):
    rows, width = shares[0].shape
    n = 2 * weights[2].shape[1]
    outs = [((2 * rows, width + 4 * n), bf16), ((8, 2 * rows), f32)]
    outs += [((rows, width), f32)] * 2
    scratch = [pltpu.VMEM((3 * n, width), bf16), pltpu.VMEM((n, width), bf16)]
    return run(
        attend_body,
        outs,
        (place, counts, *shares, *weights),
        us=6.5,
        scalars=(0, 1),
        scratch=scratch,
    )


def attend_back_body(
    place, counts, g0, g1, saved, lse, own, far, own_o, far_o, back, p0, p1, do, w, wo
):
    join_weights(own, far, own_o, far_o, w, wo)
    rows, width = g0.shape
    n = wo.shape[0]
    g = jnp.concatenate([g0[...], g1[...]], axis=0)
    back[:, :width] = g
    do[...] = dot_rt(g, wo[...]).astype(bf16)
    bias = view_bias(rows, place, counts, 0)
    attend_back_core(saved, saved, do, lse, bias, back, width, n)
    p0[...] = dot(back[:rows, width:], w[...])
    p1[...] = dot(back[rows:, width:], w[...])


def attend_back(place, counts, g, saved, lse, weights):
    rows, width = g[0].shape
    n = 2 * weights[2].shape[1]
    return run(
        attend_back_body,
        [((2 * rows, width + 3 * n), bf16)] + [((rows, width), f32)] * 2,
        (place, counts, *g, saved, lse, *weights),
        us=8.0,
        scalars=(0, 1),
        scratch=[
            pltpu.VMEM((2 * rows, n), bf16),
            pltpu.VMEM((3 * n, width), bf16),
            pltpu.VMEM((n, width), bf16),
        ],
    )


def attend_sums_body(cut, side, saved, back, near, far, *refs):
    total = refs[-1]
    width, n = near.shape
    m = n // 2
    q0, k0, v0, o0, _ = places(width, n)
    a = saved[:, :width]
    for i in range(2):
        part = dot_lt(a, back[:, q0 + i * n : q0 + (i + 1) * n])
        near[:, i * m : (i + 1) * m] = part[:, :m]
        far[:, i * m : (i + 1) * m] = part[:, m:].astype(bf16)
    for i in range(2):
        if i == 0:
            part = dot_lt(a, back[:, v0 : v0 + n])
        else:
            part = dot_lt(back[:, :width], saved[:, o0 : o0 + n])
        total[:, i * m : (i + 1) * m] = part[:, :m]
        total[:, n + i * m : n + (i + 1) * m] = part[:, m:]
    if cut:
        cut_rows(side, total, refs[0], refs[1], 0)


def attend_sums(side, peers, width, saved, back):
    n = (saved.shape[1] - width) // 4
    block = width // peers
    cut = block % 16 == 0
    outs = [((width, n), f32), ((width, n), bf16)]
    scratch = []
    if cut:
        outs += [((peers // 2, block, 2 * n), bf16), ((peers // 2, block, 2 * n), f32)]
        scratch = [pltpu.VMEM((width, 2 * n), f32)]
    else:
        outs += [((width, 2 * n), f32)]
    out = run(
        functools.partial(attend_sums_body, cut),
        outs,
        (side, saved, back),
        us=3.0,
        scalars=(0,),
        scratch=scratch,
    )
    return out if cut else (*out[:2], *cut_outside(side, peers, out[2]))


def cross_body(
    place, counts, a0, a1, a2, a3, w, wo, own, far, lse, lse_far, p0, p1, p2, p3
):
    rows, width = p0.shape
    n = wo.shape[1]
    q0, k0, v0, o0, _ = places(width, n)
    for saved, halves in ((own, (a0, a1)), (far, (a2, a3))):
        a = jnp.concatenate([halves[0][...], halves[1][...]], axis=0)
        saved[:, :width] = a
        for i, at in enumerate((q0, k0, v0)):
            saved[:, at : at + n] = dot_rt(a, w[1, i]).astype(bf16)
    attend_core(far, own, lse_far, view_bias(rows, place, counts, 0), width, n)
    p2[...] = dot(far[:rows, o0 : o0 + n], wo[1])
    p3[...] = dot(far[rows:, o0 : o0 + n], wo[1])
    attend_core(own, far, lse, view_bias(rows, place, counts, 1), width, n)
    p0[...] = dot(own[:rows, o0 : o0 + n], wo[1])
    p1[...] = dot(own[rows:, o0 : o0 + n], wo[1])


def cross(place, counts, shares, w, wo):
    rows, width = shares[0].shape
    wide = places(width, wo.shape[1])[4]
    outs = [((2 * rows, wide), bf16)] * 2 + [((8, 2 * rows), f32)] * 2
    outs += [((rows, width), f32)] * 4
    args = (place, counts, *shares, w, wo)
    return run(cross_body, outs, args, us=6.5, scalars=(0, 1))


def cross_back_body(other, place, counts, g0, g1, from_q, from_k, lse, wo, back, do):
    rows, width = g0.shape
    n = wo.shape[1]
    g = jnp.concatenate([g0[...], g1[...]], axis=0)
    back[:, :width] = g
    do[...] = dot_rt(g, wo[1]).astype(bf16)
    bias = view_bias(rows, place, counts, other)
    attend_back_core(from_q, from_k, do, lse, bias, back, width, n)


def cross_back(other, place, counts, g, from_q, from_k, lse, wo):
    rows, width = g[0].shape
    n = wo.shape[1]
    return run(
        functools.partial(cross_back_body, other),
        [((2 * rows, places(width, n)[3]), bf16)],
        (place, counts, *g, from_q, from_k, lse, wo),
        us=4.0,
        scalars=(0, 1),
        scratch=[pltpu.VMEM((2 * rows, n), bf16)],
    )[0]


def cross_rows_body(own, far, w, p0, p1, p2, p3):
    rows, width = p0.shape
    n = w.shape[2]
    q0, k0, v0, _, _ = places(width, n)
    for queries, keys, parts in ((far, own, (p2, p3)), (own, far, (p0, p1))):
        for i, part in enumerate(parts):
            at = slice(i * rows, (i + 1) * rows)
            part[...] = (
                dot(queries[at, q0 : q0 + n], w[1, 0])
                + dot(keys[at, k0 : k0 + n], w[1, 1])
                + dot(keys[at, v0 : v0 + n], w[1, 2])
            )


def cross_rows(rows, width, own, far, w):
    return run(cross_rows_body, [((rows, width), f32)] * 4, (own, far, w), us=2.0)


def cross_sums_body(own, far, own_back, far_back, sums):
    width = sums.shape[0]
    n = sums.shape[1] // 4
    q0, k0, v0, o0, _ = places(width, n)
    rows = lambda first, second, at, size: jnp.concatenate(
        [first[:, at : at + size], second[:, at : at + size]], axis=0
    )
    queries = rows(own, far, 0, width)
    keys = rows(far, own, 0, width)
    parts = [
        (queries, rows(own_back, far_back, q0, n)),
        (keys, rows(own_back, far_back, k0, n)),
        (keys, rows(own_back, far_back, v0, n)),
        (rows(own_back, far_back, 0, width), rows(own, far, o0, n)),
    ]
    for i, (left, right) in enumerate(parts):
        sums[:, i * n : (i + 1) * n] = dot_lt(left, right).astype(bf16)


def cross_sums(width, n, own, far, own_back, far_back):
    return run(
        cross_sums_body, [((width, 4 * n), bf16)], (own, far, own_back, far_back), us=3.0
    )[0]


def on_device(
    tokens,
    cotangent,
    mix_coef,
    partner_dev,
    partner_row,
    view_counts,
    w_qkv,
    w_out,
    w_up,
    w_down,
    gain_attn,
    gain_mlp,
):
    peers = lax.axis_size("dp")
    rows = mix_coef.shape[0]
    width = tokens.shape[1]
    mine = w_qkv.shape[-1]
    block = width // peers
    capacity = max(2, 2 * rows // peers)
    slots = peers * capacity
    place = lax.axis_index("mp").astype(i32)[None]
    side = (lax.axis_index("dp") % 2).astype(i32)[None]
    weight_own = mix_coef[:, None]

    slot, requests = run(
        functools.partial(ask_body, capacity),
        [((1, rows), i32), ((peers, capacity), i32)],
        (partner_dev.reshape(1, rows), partner_row.reshape(1, rows)),
    )

    own_w = w_qkv.transpose(0, 2, 3, 1)
    far_o = swap_view(w_out[:1])
    far_w = swap_view(own_w[:1])
    asked = lax.all_to_all(requests, "dp", split_axis=0, concat_axis=0, tiled=True)
    asked = after(asked, far_o).reshape(1, slots)
    (found,) = run(find_body, [((slots, width), bf16)], (asked, tokens), us=2.0)
    replies = lax.all_to_all(
        found.reshape(peers, capacity, width), "dp", split_axis=0, concat_axis=0, tiled=True
    )
    own_tokens = lax.dynamic_slice_in_dim(tokens, place[0] * rows, rows, 0)
    replies, far_w, own_tokens = lax.optimization_barrier((replies, far_w, own_tokens))
    stream, a_share = run(
        mix_body,
        [((rows, width), f32), ((rows, width), bf16)],
        (slot, replies.reshape(slots, width), own_tokens, weight_own, gain_attn[:1]),
        us=1.5,
    )
    mlp_w = (w_up, swap_core(w_up), w_down, swap_core(w_down))

    def feed_forward(layer, b_share):
        b_far = swap_view(b_share)
        own, own_core, slope_own, part = mlp(layer, b_share, mlp_w, f32)
        far, far_core, slope_far, there = mlp(layer, after(b_far, part), mlp_w, bf16)
        kept = (own, swap_core(own_core), far, swap_core(far_core))
        return kept, (slope_own, slope_far), (part, swap_view(there))

    def feed_forward_back(layer, g_share, kept, slope, due=()):
        g_far = swap_view(g_share)
        own, own_core, part = mlp_back(layer, g_share, slope[0], mlp_w, f32)
        g_far = after(g_far, part)
        far, far_core, there = mlp_back(layer, g_far, slope[1], mlp_w, bf16)
        arrived = swap_view(there)
        if layer == 0:
            arrived = after(arrived, got_attn1)
        back = (own, swap_core(own_core), far, swap_core(far_core))
        sums = mlp_sums(width, kept, after(back, *due))
        return sums, (part, after(arrived, sums))

    first_in = stream
    weights = (own_w[:1], far_w, w_out[:1], far_o)
    kept0, lse0, part, part_core = attend(place, view_counts, (a_share, swap_core(a_share)), weights)
    first_mid, b_share = join_norm(first_in, (part, swap_core(part_core)), gain_mlp[0])
    mlp0, slope0, terms = feed_forward(0, b_share)

    second_in, a_share = join_norm(first_mid, terms, gain_attn[1])
    a_far = swap_view(a_share)
    shares = (a_share, swap_core(a_share), a_far, swap_core(a_far))
    own1, far1, lse1, lse1_far, part, part_core, there, there_core = cross(
        place, view_counts, shares, own_w, w_out
    )
    arrived = swap_view((there + swap_core(there_core)).astype(bf16))
    second_mid, b_share = join_norm(second_in, (part, swap_core(part_core), arrived), gain_mlp[1])
    mlp1, slope1, terms = feed_forward(1, b_share)
    layer_output = (second_mid + terms[0] + terms[1].astype(f32)).astype(bf16)

    def along_z(values):
        groups = [list(range(s, peers, 2)) for s in range(2)]
        return lax.psum_scatter(
            values, "dp", scatter_dimension=0, tiled=True, axis_index_groups=groups
        )

    def between_sides(values):
        send = lax.dynamic_slice_in_dim(values, (1 - side[0]) * block, block, 0)
        keep = lax.dynamic_slice_in_dim(values, side[0] * block, block, 0)
        return keep.astype(f32) + swap_side(send).astype(f32)

    gain_parts = [None] * 4
    mlp_sum1, terms = feed_forward_back(1, cotangent, mlp1, slope1)
    sum_mlp1 = along_z(mlp_sum1)
    gain_parts[3], gradient, g_share = norm_back(second_mid, gain_mlp[1], cotangent, terms)

    g_far = swap_view(g_share)
    own_back = cross_back(
        1, place, view_counts, (g_share, swap_core(g_share)), own1, far1, lse1, w_out
    )
    g_far = after(g_far, own_back)
    far_back = cross_back(
        0, place, view_counts, (g_far, swap_core(g_far)), far1, own1, lse1_far, w_out
    )
    part, part_core, there, there_core = cross_rows(rows, width, own_back, far_back, own_w)
    arrived = swap_view((there + swap_core(there_core)).astype(bf16))
    attn_sum1 = cross_sums(width, mine, own1, far1, own_back, far_back)
    terms = (part, swap_core(part_core), after(arrived, attn_sum1))
    attn_cut = cut_outside(side, peers, attn_sum1)
    got_attn1 = swap_side(attn_cut[0])
    gain_parts[1], gradient, g_share = norm_back(second_in, gain_attn[1], gradient, terms)

    mlp_sum0, terms = feed_forward_back(0, g_share, mlp0, slope0)
    sum_mlp0 = along_z(after(mlp_sum0, sum_mlp1))
    gain_parts[2], gradient, g_share = norm_back(first_mid, gain_mlp[0], gradient, terms)

    back, part, part_core = attend_back(
        place, view_counts, (g_share, swap_core(g_share)), kept0, lse0, weights
    )
    back, layer_output = lax.optimization_barrier((back, layer_output))
    near, far, send, keep = attend_sums(side, peers, width, kept0, back)
    gain_parts[0], gradient, _ = norm_back(
        first_in, gain_attn[0], gradient, (part, swap_core(part_core))
    )

    (outgoing,) = run(
        give_body,
        [((peers, capacity + 8, width), bf16)],
        (slot, weight_own, gradient, *gain_parts),
        us=1.5,
    )
    returned = lax.all_to_all(outgoing, "dp", split_axis=0, concat_axis=0, tiled=True)

    got_far, got_send, _ = lax.optimization_barrier((swap_view(far), swap_side(send), outgoing))
    send_qk, keep_qk = cut_outside(side, peers, near + got_far.astype(f32))
    keep_vo = keep + got_send.astype(f32)
    n = near.shape[1]
    sum_qk = (keep_qk + swap_side(send_qk).astype(f32)).astype(bf16)
    sum_vo = (keep_vo[:, :, :n] + swap_view(keep_vo[:, :, n:].astype(bf16)).astype(f32)).astype(bf16)
    first_sum = (attn_cut[1].astype(f32) + got_attn1.astype(f32)).astype(bf16)
    joined = jnp.concatenate([sum_qk, sum_vo, first_sum], axis=2)
    joined = joined.reshape(peers // 2 * block, 8 * mine)
    joined, sum_mlp0, returned = lax.optimization_barrier((joined, sum_mlp0, returned))
    attn_sum = along_z(joined)
    mlp_all = jnp.stack([between_sides(sum_mlp0), between_sides(sum_mlp1)])
    gain_sum, part, part_core, there, there_core = run(
        spread_body,
        [((4, width), f32)] + [((rows, width), f32)] * 4,
        (place, asked, returned),
        us=1.5,
        scalars=(0,),
        scratch=[pltpu.VMEM((slots, width), bf16)],
    )
    gain_sum = gain_sum + swap_core(gain_sum)
    gain_sum = gain_sum + swap_view(gain_sum)
    gain_sum = lax.dynamic_slice_in_dim(gain_sum, lax.axis_index("dp") * block, block, 1)
    arrived = swap_view((there + swap_core(there_core)).astype(bf16))
    grad_tokens = weight_own * gradient + part + swap_core(part_core) + arrived.astype(f32)

    grad_qkv, grad_out = run(
        finish_body, [((2, 3, block, mine), f32), ((2, mine, block), f32)], (attn_sum,)
    )
    hidden = mlp_all.shape[-1] // 2
    return (
        layer_output,
        grad_tokens,
        grad_qkv.transpose(0, 2, 1, 3),
        grad_out,
        mlp_all[:, :, :hidden],
        mlp_all[:, :, hidden:].transpose(0, 2, 1),
        gain_sum[:2],
        gain_sum[2:],
    )


def solution(mesh):
    placed = (
        P("dp", None),
        P(("dp", "mp"), None),
        P(("dp", "mp")),
        P(("dp", "mp"), None),
        P(("dp", "mp")),
        P("dp", None),
        P(None, None, None, "mp"),
        P(None, "mp", None),
        P(None, None, "mp"),
        P(None, "mp", None),
        P(),
        P(),
    )
    return jax.shard_map(
        on_device,
        mesh=mesh,
        in_specs=placed,
        out_specs=(
            P(("dp", "mp"), None),
            P(("dp", "mp"), None),
            P(None, "dp", None, "mp"),
            P(None, "mp", "dp"),
            P(None, "dp", "mp"),
            P(None, "mp", "dp"),
            P(None, "dp"),
            P(None, "dp"),
        ),
        check_vma=False,
    )
```

```python
import functools

import jax
import jax.numpy as jnp
from jax import lax
from jax.experimental import pallas as pl
from jax.experimental.pallas import tpu as pltpu
from jax.sharding import PartitionSpec as P

HD = 64
SCALE = HD ** (-0.5)
epsilon = 1e-06
masked_score = -1000000000.0
bf16 = jnp.bfloat16
f32 = jnp.float32
i32 = jnp.int32

TAIL_P = 0.38
TAIL = (
    0.2144098248509563,
    0.21394460416600933,
    0.20368405029440034,
    0.13968567743708352,
    0.2272053511927878,
    -0.15681775904774625,
    0.3593185352386043,
    -0.25984971762641107,
    0.058419421394547984,
)


def dot(left, right):
    return jnp.dot(left, right, preferred_element_type=f32)


def dot_rt(left, right):
    return lax.dot_general(left, right, (((1,), (1,)), ((), ())), preferred_element_type=f32)


def dot_lt(left, right):
    return lax.dot_general(left, right, (((0,), (0,)), ((), ())), preferred_element_type=f32)


def swap_core(values):
    return lax.ppermute(values, "mp", [(i, i ^ 1) for i in range(4)])


def swap_view(values):
    return lax.ppermute(values, "mp", [(i, i ^ 2) for i in range(4)])


def swap_side(values):
    return lax.ppermute(values, "dp", [(i, i ^ 1) for i in range(lax.axis_size("dp"))])


def after(values, *others):
    return lax.optimization_barrier((values, *others))[0]


def run(body, outs, args, us=1.0, scalars=(), scratch=(), hidden=False, left=()):
    return pl.pallas_call(
        body,
        out_shape=[jax.ShapeDtypeStruct(s, d) for s, d in outs],
        in_specs=[
            pl.BlockSpec(
                memory_space=pltpu.SMEM if i in scalars else pl.ANY if i in left else pltpu.VMEM
            )
            for i in range(len(args))
        ],
        out_specs=[pl.BlockSpec(memory_space=pltpu.VMEM) for _ in outs],
        scratch_shapes=list(scratch),
        compiler_params=pltpu.CompilerParams(vmem_limit_bytes=VMEM_LIMIT),
        cost_estimate=pl.CostEstimate(
            flops=int(us * PEAK * (3 if hidden else 1)), bytes_accessed=0, transcendentals=0
        ),
    )(*args)


VMEM_LIMIT = 16 * 1024 * 1024
PEAK = 1.15e9


def norm_parts(values):
    centred = values - jnp.mean(values, axis=-1, keepdims=True)
    rstd = lax.rsqrt(jnp.mean(centred * centred, axis=-1, keepdims=True) + epsilon)
    return centred * rstd, rstd


def join_body(count, *refs):
    base, terms, gain = refs[0], refs[1 : 1 + count], refs[1 + count]
    total = base[...]
    for term in terms:
        total = total + term[...].astype(f32)
    refs[2 + count][...] = total
    refs[3 + count][...] = (norm_parts(total)[0] * gain[...]).astype(bf16)


def join_norm(base, terms, gain):
    outs = [(base.shape, f32), (base.shape, bf16)]
    body = functools.partial(join_body, len(terms))
    return run(body, outs, (base, *terms, gain[None]), us=1.1)


def norm_back_body(count, *refs):
    values, gain, gradient = refs[:3]
    total = refs[3][...].astype(f32)
    for term in refs[4 : 3 + count]:
        total = total + term[...].astype(f32)
    n, rstd = norm_parts(values[...])
    refs[3 + count][...] = jnp.sum(total * n, axis=0, keepdims=True)
    dn = total * gain[...]
    dx = rstd * (
        dn - jnp.mean(dn, axis=-1, keepdims=True) - n * jnp.mean(dn * n, axis=-1, keepdims=True)
    )
    new = gradient[...].astype(f32) + dx
    refs[4 + count][...] = new
    refs[5 + count][...] = new.astype(bf16)


def norm_back(values, gain, gradient, terms):
    outs = [((1, values.shape[1]), f32), (values.shape, f32), (values.shape, bf16)]
    body = functools.partial(norm_back_body, len(terms))
    return run(body, outs, (values, gain[None], gradient, *terms), us=1.5)


def finish_body(sums, qkv, out):
    m = out.shape[1]
    for layer in range(2):
        at = 4 * m * layer
        for i in range(3):
            qkv[layer, i] = sums[:, at + i * m : at + (i + 1) * m].astype(f32)
        out[layer] = sums[:, at + 3 * m : at + 4 * m].astype(f32).T


def ask_body(capacity, target, partner, slot_ref, ask_ref):
    peers = ask_ref.shape[0]
    rows = target.shape[1]
    chosen = lax.broadcasted_iota(i32, (peers, rows), 0) == target[...]
    earlier = lax.broadcasted_iota(i32, (rows, rows), 0) < lax.broadcasted_iota(
        i32, (rows, rows), 1
    )
    before = dot(jnp.where(chosen, 1.0, 0.0).astype(bf16), jnp.where(earlier, 1.0, 0.0).astype(bf16))
    rank = jnp.sum(jnp.where(chosen, before, 0.0), axis=0, keepdims=True).astype(i32)
    slot_ref[...] = target[...] * capacity + rank
    placed = lax.broadcasted_iota(i32, (capacity, rows), 0) == rank
    placed = jnp.where(placed, 1.0, 0.0).astype(bf16)
    high = partner[...] // 32
    low = partner[...] - high * 32
    part = lambda v: dot_rt(jnp.where(chosen, v.astype(f32), 0.0).astype(bf16), placed)
    ask_ref[...] = (part(high) * 32.0 + part(low)).astype(i32)


def one_hot(index, count):
    hit = lax.broadcasted_iota(i32, (count, index.shape[1]), 0) == index[...]
    return jnp.where(hit, 1.0, 0.0).astype(bf16)


def find_body(asked, tokens, found):
    found[...] = dot_lt(one_hot(asked, tokens.shape[0]), tokens[...]).astype(bf16)


def column(row):
    return jnp.broadcast_to(row[...], (8, row.shape[1])).T[:, :1]


def mix_body(place, slot, replies, tokens, weight, gain, stream, normed, own, sem):
    rows = own.shape[0]
    start = pl.multiple_of(place[0] * rows, rows)
    copy = pltpu.make_async_copy(tokens.at[pl.ds(start, rows), :], own, sem)
    copy.start()
    partner = dot_lt(one_hot(slot, replies.shape[0]), replies[...])
    mine = column(weight)
    copy.wait()
    total = mine * own[...].astype(f32) + (1.0 - mine) * partner
    stream[...] = total
    normed[...] = (norm_parts(total)[0] * gain[...]).astype(bf16)


def give_body(slot, weight, gradient, g0, g1, g2, g3, outgoing):
    peers, count, _ = outgoing.shape
    capacity = count - 8
    rows = ((1.0 - column(weight)) * gradient[...]).astype(bf16)
    placed = dot(one_hot(slot, peers * capacity), rows).astype(bf16)
    gains = jnp.concatenate([g0[...], g1[...], g2[...], g3[...]], axis=0)
    high = gains.astype(bf16)
    extra = jnp.concatenate([high.astype(f32), gains - high.astype(f32)], axis=0).astype(bf16)
    for p in range(peers):
        outgoing[p, :capacity, :] = placed[p * capacity : (p + 1) * capacity, :]
        outgoing[p, capacity:, :] = extra


def spread_body(place, asked, returned, gains, *refs):
    near, core, far, far_core, flat = refs
    peers, count, _ = returned.shape
    capacity = count - 8
    rows = near.shape[0]
    total = jnp.zeros((8, near.shape[1]), f32)
    for p in range(peers):
        flat[p * capacity : (p + 1) * capacity, :] = returned[p, :capacity, :]
        total = total + returned[p, capacity:, :].astype(f32)
    gains[...] = total[:4] + total[4:]
    for i, ref in enumerate((near, core, far, far_core)):
        owner = jnp.bitwise_xor(place[0], i)
        ref[...] = dot(one_hot(asked[...] - owner * rows, rows), flat[...])


def gelu_parts(u):
    t = 1.0 / (1.0 + (TAIL_P * 0.5**0.5) * jnp.abs(u))
    poly = TAIL[-1]
    for c in TAIL[-2::-1]:
        poly = poly * t + c
    bell = jnp.exp(-0.5 * u * u)
    tail = 0.5 * poly * t * bell
    phi = jnp.where(u < 0.0, tail, 1.0 - tail)
    return u * phi, phi + u * bell * 0.3989422804014327


def fetch(layer, sources, places, sems):
    copies = [
        pltpu.make_async_copy(source.at[layer], place, sems.at[i])
        for i, (source, place) in enumerate(zip(sources, places))
    ]
    for copy in copies:
        copy.start()
    return copies


def mlp_body(layer, b, up0, up1, down0, down1, mine, theirs, slope, part, up2, down2, sems):
    width = b.shape[1]
    hidden = up0.shape[2]
    rows = b[...]
    copies = fetch(layer, (up1, down1), (up2, down2), sems)
    total = 0.0
    sides = ((mine, up0.at[layer], down0.at[layer]), (theirs, up2, down2))
    for i, (saved, up, down) in enumerate(sides):
        saved[:, :width] = rows
        if i == 1:
            for copy in copies:
                copy.wait()
        for j in range(0, hidden, 256):
            z, dz = gelu_parts(dot(rows, up[:, j : j + 256]))
            saved[:, width + j : width + j + 256] = z.astype(bf16)
            slope[:, i * hidden + j : i * hidden + j + 256] = dz
        total = total + dot(saved[:, width:], down[...])
    part[...] = total.astype(part.dtype)


def fetched(weights):
    shapes = [pltpu.VMEM(w.shape[1:], w.dtype) for w in (weights[1], weights[3])]
    return [*shapes, pltpu.SemaphoreType.DMA((2,))]


def mlp(layer, b, weights, dtype):
    rows, width = b.shape
    hidden = weights[0].shape[2]
    outs = [((rows, width + hidden), bf16)] * 2
    outs += [((rows, 2 * hidden), f32), ((rows, width), dtype)]
    body = functools.partial(mlp_body, layer)
    return run(body, outs, (b, *weights), us=3.5, scratch=fetched(weights), left=(2, 4))


def mlp_back_body(
    layer, g, slope, up0, up1, down0, down1, mine, theirs, part, up2, down2, sems
):
    width = g.shape[1]
    hidden = up0.shape[2]
    rows = g[...]
    copies = fetch(layer, (up1, down1), (up2, down2), sems)
    total = 0.0
    sides = ((mine, up0.at[layer], down0.at[layer]), (theirs, up2, down2))
    for i, (saved, up, down) in enumerate(sides):
        saved[:, :width] = rows
        if i == 1:
            for copy in copies:
                copy.wait()
        for j in range(0, hidden, 256):
            at = i * hidden + j
            dz = dot_rt(rows, down[j : j + 256, :])
            saved[:, width + j : width + j + 256] = (dz * slope[:, at : at + 256]).astype(bf16)
        total = total + dot_rt(saved[:, width:], up[...])
    part[...] = total.astype(part.dtype)


def mlp_back(layer, g, slope, weights, dtype):
    rows, width = g.shape
    hidden = weights[0].shape[2]
    outs = [((rows, width + hidden), bf16)] * 2 + [((rows, width), dtype)]
    body = functools.partial(mlp_back_body, layer)
    return run(body, outs, (g, slope, *weights), us=2.5, scratch=fetched(weights), left=(3, 5))


def mlp_sums_body(*refs):
    ahead, back, sums = refs[:4], refs[4:8], refs[8]
    width = sums.shape[0]
    hidden = sums.shape[1] // 2
    for i, (left, right) in enumerate(((ahead, back), (back, ahead))):
        left = jnp.concatenate([v[:, :width] for v in left], axis=0)
        right = jnp.concatenate([v[:, width:] for v in right], axis=0)
        sums[:, i * hidden : (i + 1) * hidden] = dot_lt(left, right).astype(bf16)


def mlp_sums(width, ahead, back):
    outs = [((width, 2 * (ahead[0].shape[1] - width)), bf16)]
    return run(mlp_sums_body, outs, (*ahead, *back), us=3.5, hidden=True)[0]


def cut_rows(side, values, send, keep, column):
    count, block, _ = send.shape
    n = values.shape[1]
    for z in range(count):
        theirs = pl.multiple_of((2 * z + 1 - side[0]) * block, 8)
        mine = pl.multiple_of((2 * z + side[0]) * block, 8)
        send[z, :, column : column + n] = values[pl.ds(theirs, block), :].astype(bf16)
        keep[z, :, column : column + n] = values[pl.ds(mine, block), :]


def cut_outside(side, peers, grads):
    parts = grads.reshape(peers // 2, 2, -1, grads.shape[1])
    send = lax.dynamic_index_in_dim(parts, 1 - side[0], 1, False)
    return send.astype(bf16), lax.dynamic_index_in_dim(parts, side[0], 1, False)


def groups_of(n):
    return [(j, min(128, n - j)) for j in range(0, n, 128)]


def places(width, n):
    stride = -(-n // 128) * 128
    return [width + i * stride for i in range(5)]


def view_bias(rows, place, counts, other):
    half = lax.rem(place[0], 2)
    count = counts[0, jnp.bitwise_xor(lax.div(place[0], 2), other)]
    index = lax.broadcasted_iota(i32, (2 * rows, 1), 0)
    position = jnp.where(index < rows, index + half * rows, index - half * rows)
    return jnp.where(position < count, 0.0, masked_score).astype(f32)


def masked(values, head):
    if values.shape[1] == HD:
        return values
    keep = lax.broadcasted_iota(i32, values.shape, 1) // HD == head
    return jnp.where(keep, values, jnp.zeros_like(values))


def attend_core(from_q, from_k, lse, bias, width, n):
    q0, k0, v0, o0, _ = places(width, n)
    lse[...] = jnp.zeros(lse.shape, f32)
    for j, w in groups_of(n):
        q = from_q[:, q0 + j : q0 + j + w] * jnp.asarray(SCALE, bf16)
        k = from_k[:, k0 + j : k0 + j + w]
        v = from_k[:, v0 + j : v0 + j + w]
        out = jnp.zeros((w, q.shape[0]), f32)
        for head in range(w // HD):
            s = dot_rt(k, masked(q, head)) + bias
            top = jnp.max(s, axis=0, keepdims=True)
            e = jnp.exp(s - top)
            total = jnp.sum(e, axis=0, keepdims=True)
            weights = (e * (1.0 / total)).astype(bf16)
            at = j // HD + head
            lse[at : at + 1, :] = top + jnp.log(total)
            out = out + dot_lt(masked(v, head), weights)
        from_q[:, o0 + j : o0 + j + w] = out.T.astype(bf16)


def attend_back_core(from_q, from_k, do, lse, bias, back, width, n):
    q0, k0, v0, _, _ = places(width, n)
    for j, w in groups_of(n):
        q = from_q[:, q0 + j : q0 + j + w] * jnp.asarray(SCALE, bf16)
        k = from_k[:, k0 + j : k0 + j + w]
        v = from_k[:, v0 + j : v0 + j + w]
        d = do[:, j : j + w]
        dv = jnp.zeros(q.shape, f32)
        dk = jnp.zeros(q.shape, f32)
        dq = jnp.zeros((w, q.shape[0]), f32)
        for head in range(w // HD):
            qm, dm, km = masked(q, head), masked(d, head), masked(k, head)
            at = j // HD + head
            p = jnp.exp(dot_rt(k, qm) + bias - lse[at : at + 1, :])
            dp = dot_rt(v, dm)
            centre = jnp.sum(p * dp, axis=0, keepdims=True)
            ds = (p * (dp - centre)).astype(bf16)
            dv = dv + dot(p.astype(bf16), dm)
            dk = dk + dot(ds, qm)
            dq = dq + dot_lt(km, ds)
        back[:, q0 + j : q0 + j + w] = (dq.T * SCALE).astype(bf16)
        back[:, k0 + j : k0 + j + w] = dk.astype(bf16)
        back[:, v0 + j : v0 + j + w] = dv.astype(bf16)


def join_weights(own, far, own_o, far_o, w, wo):
    m = own_o.shape[1]
    for i in range(3):
        w[2 * i * m : (2 * i + 1) * m, :] = own[0, i]
        w[(2 * i + 1) * m : (2 * i + 2) * m, :] = far[0, i]
    wo[:m, :] = own_o[0]
    wo[m:, :] = far_o[0]


def attend_body(place, counts, a0, a1, own, far, own_o, far_o, saved, lse, p0, p1, w, wo):
    join_weights(own, far, own_o, far_o, w, wo)
    rows, width = p0.shape
    n = wo.shape[0]
    q0, _, _, o0, _ = places(width, n)
    a = jnp.concatenate([a0[...], a1[...]], axis=0)
    saved[:, :width] = a
    saved[:, q0:o0] = dot_rt(a, w[...]).astype(bf16)
    attend_core(saved, saved, lse, view_bias(rows, place, counts, 0), width, n)
    p0[...] = dot(saved[:rows, o0:], wo[...])
    p1[...] = dot(saved[rows:, o0:], wo[...])


def attend(place, counts, shares, weights):
    rows, width = shares[0].shape
    n = 2 * weights[2].shape[1]
    outs = [((2 * rows, width + 4 * n), bf16), ((8, 2 * rows), f32)]
    outs += [((rows, width), f32)] * 2
    scratch = [pltpu.VMEM((3 * n, width), bf16), pltpu.VMEM((n, width), bf16)]
    return run(
        attend_body,
        outs,
        (place, counts, *shares, *weights),
        us=6.5,
        scalars=(0, 1),
        scratch=scratch,
    )


def attend_back_body(
    place, counts, g0, g1, saved, lse, own, far, own_o, far_o, back, p0, p1, do, w, wo
):
    join_weights(own, far, own_o, far_o, w, wo)
    rows, width = g0.shape
    n = wo.shape[0]
    g = jnp.concatenate([g0[...], g1[...]], axis=0)
    back[:, :width] = g
    do[...] = dot_rt(g, wo[...]).astype(bf16)
    bias = view_bias(rows, place, counts, 0)
    attend_back_core(saved, saved, do, lse, bias, back, width, n)
    p0[...] = dot(back[:rows, width:], w[...])
    p1[...] = dot(back[rows:, width:], w[...])


def attend_back(place, counts, g, saved, lse, weights):
    rows, width = g[0].shape
    n = 2 * weights[2].shape[1]
    return run(
        attend_back_body,
        [((2 * rows, width + 3 * n), bf16)] + [((rows, width), f32)] * 2,
        (place, counts, *g, saved, lse, *weights),
        us=8.0,
        scalars=(0, 1),
        scratch=[
            pltpu.VMEM((2 * rows, n), bf16),
            pltpu.VMEM((3 * n, width), bf16),
            pltpu.VMEM((n, width), bf16),
        ],
    )


def attend_sums_body(cut, side, saved, back, near, far, *refs):
    total = refs[-1]
    width, n = near.shape
    m = n // 2
    q0, k0, v0, o0, _ = places(width, n)
    a = saved[:, :width]
    for i in range(2):
        part = dot_lt(a, back[:, q0 + i * n : q0 + (i + 1) * n])
        near[:, i * m : (i + 1) * m] = part[:, :m]
        far[:, i * m : (i + 1) * m] = part[:, m:].astype(bf16)
    for i in range(2):
        if i == 0:
            part = dot_lt(a, back[:, v0 : v0 + n])
        else:
            part = dot_lt(back[:, :width], saved[:, o0 : o0 + n])
        total[:, i * m : (i + 1) * m] = part[:, :m]
        total[:, n + i * m : n + (i + 1) * m] = part[:, m:]
    if cut:
        cut_rows(side, total, refs[0], refs[1], 0)


def attend_sums(side, peers, width, saved, back):
    n = (saved.shape[1] - width) // 4
    block = width // peers
    cut = block % 16 == 0
    outs = [((width, n), f32), ((width, n), bf16)]
    scratch = []
    if cut:
        outs += [((peers // 2, block, 2 * n), bf16), ((peers // 2, block, 2 * n), f32)]
        scratch = [pltpu.VMEM((width, 2 * n), f32)]
    else:
        outs += [((width, 2 * n), f32)]
    out = run(
        functools.partial(attend_sums_body, cut),
        outs,
        (side, saved, back),
        us=3.0,
        scalars=(0,),
        scratch=scratch,
    )
    return out if cut else (*out[:2], *cut_outside(side, peers, out[2]))


def cross_body(
    place, counts, a0, a1, a2, a3, w, wo, own, far, lse, lse_far, p0, p1, p2, p3
):
    rows, width = p0.shape
    n = wo.shape[1]
    q0, k0, v0, o0, _ = places(width, n)
    for saved, halves in ((own, (a0, a1)), (far, (a2, a3))):
        a = jnp.concatenate([halves[0][...], halves[1][...]], axis=0)
        saved[:, :width] = a
        for i, at in enumerate((q0, k0, v0)):
            saved[:, at : at + n] = dot_rt(a, w[1, i]).astype(bf16)
    attend_core(far, own, lse_far, view_bias(rows, place, counts, 0), width, n)
    p2[...] = dot(far[:rows, o0 : o0 + n], wo[1])
    p3[...] = dot(far[rows:, o0 : o0 + n], wo[1])
    attend_core(own, far, lse, view_bias(rows, place, counts, 1), width, n)
    p0[...] = dot(own[:rows, o0 : o0 + n], wo[1])
    p1[...] = dot(own[rows:, o0 : o0 + n], wo[1])


def cross(place, counts, shares, w, wo):
    rows, width = shares[0].shape
    wide = places(width, wo.shape[1])[4]
    outs = [((2 * rows, wide), bf16)] * 2 + [((8, 2 * rows), f32)] * 2
    outs += [((rows, width), f32)] * 4
    args = (place, counts, *shares, w, wo)
    return run(cross_body, outs, args, us=6.5, scalars=(0, 1))


def cross_back_body(other, place, counts, g0, g1, from_q, from_k, lse, wo, back, do):
    rows, width = g0.shape
    n = wo.shape[1]
    g = jnp.concatenate([g0[...], g1[...]], axis=0)
    back[:, :width] = g
    do[...] = dot_rt(g, wo[1]).astype(bf16)
    bias = view_bias(rows, place, counts, other)
    attend_back_core(from_q, from_k, do, lse, bias, back, width, n)


def cross_back(other, place, counts, g, from_q, from_k, lse, wo):
    rows, width = g[0].shape
    n = wo.shape[1]
    return run(
        functools.partial(cross_back_body, other),
        [((2 * rows, places(width, n)[3]), bf16)],
        (place, counts, *g, from_q, from_k, lse, wo),
        us=4.0,
        scalars=(0, 1),
        scratch=[pltpu.VMEM((2 * rows, n), bf16)],
    )[0]


def cross_rows_body(own, far, w, p0, p1, p2, p3):
    rows, width = p0.shape
    n = w.shape[2]
    q0, k0, v0, _, _ = places(width, n)
    for queries, keys, parts in ((far, own, (p2, p3)), (own, far, (p0, p1))):
        for i, part in enumerate(parts):
            at = slice(i * rows, (i + 1) * rows)
            part[...] = (
                dot(queries[at, q0 : q0 + n], w[1, 0])
                + dot(keys[at, k0 : k0 + n], w[1, 1])
                + dot(keys[at, v0 : v0 + n], w[1, 2])
            )


def cross_rows(rows, width, own, far, w):
    return run(cross_rows_body, [((rows, width), f32)] * 4, (own, far, w), us=2.0)


def cross_sums_body(own, far, own_back, far_back, sums):
    width = sums.shape[0]
    n = sums.shape[1] // 4
    q0, k0, v0, o0, _ = places(width, n)
    rows = lambda first, second, at, size: jnp.concatenate(
        [first[:, at : at + size], second[:, at : at + size]], axis=0
    )
    queries = rows(own, far, 0, width)
    keys = rows(far, own, 0, width)
    parts = [
        (queries, rows(own_back, far_back, q0, n)),
        (keys, rows(own_back, far_back, k0, n)),
        (keys, rows(own_back, far_back, v0, n)),
        (rows(own_back, far_back, 0, width), rows(own, far, o0, n)),
    ]
    for i, (left, right) in enumerate(parts):
        sums[:, i * n : (i + 1) * n] = dot_lt(left, right).astype(bf16)


def cross_sums(width, n, own, far, own_back, far_back):
    return run(
        cross_sums_body, [((width, 4 * n), bf16)], (own, far, own_back, far_back), us=3.0
    )[0]


def on_device(
    tokens,
    cotangent,
    mix_coef,
    partner_dev,
    partner_row,
    view_counts,
    w_qkv,
    w_out,
    w_up,
    w_down,
    gain_attn,
    gain_mlp,
):
    peers = lax.axis_size("dp")
    rows = mix_coef.shape[0]
    width = tokens.shape[1]
    mine = w_qkv.shape[-1]
    block = width // peers
    capacity = max(2, 2 * rows // peers)
    slots = peers * capacity
    place = lax.axis_index("mp").astype(i32)[None]
    side = (lax.axis_index("dp") % 2).astype(i32)[None]
    weight_own = mix_coef[:, None]
    weight_row = mix_coef[None]

    slot, requests = run(
        functools.partial(ask_body, capacity),
        [((1, rows), i32), ((peers, capacity), i32)],
        (partner_dev.reshape(1, rows), partner_row.reshape(1, rows)),
    )

    own_w = w_qkv.transpose(0, 2, 3, 1)
    far_o = swap_view(w_out[:1])
    far_w = swap_view(own_w[:1])
    asked = lax.all_to_all(requests, "dp", split_axis=0, concat_axis=0, tiled=True)
    asked = after(asked, far_o).reshape(1, slots)
    (found,) = run(find_body, [((slots, width), bf16)], (asked, tokens), us=2.0)
    replies = lax.all_to_all(
        found.reshape(peers, capacity, width), "dp", split_axis=0, concat_axis=0, tiled=True
    )
    replies, far_w = lax.optimization_barrier((replies, far_w))
    stream, a_share = run(
        mix_body,
        [((rows, width), f32), ((rows, width), bf16)],
        (place, slot, replies.reshape(slots, width), tokens, weight_row, gain_attn[:1]),
        us=1.5,
        scalars=(0,),
        left=(3,),
        scratch=[pltpu.VMEM((rows, width), tokens.dtype), pltpu.SemaphoreType.DMA],
    )
    mlp_w = (w_up, swap_core(w_up), w_down, swap_core(w_down))

    def feed_forward(layer, b_share):
        b_far = swap_view(b_share)
        own, own_core, slope_own, part = mlp(layer, b_share, mlp_w, f32)
        far, far_core, slope_far, there = mlp(layer, after(b_far, part), mlp_w, bf16)
        kept = (own, swap_core(own_core), far, swap_core(far_core))
        return kept, (slope_own, slope_far), (part, swap_view(there))

    def feed_forward_back(layer, g_share, kept, slope, due=()):
        g_far = swap_view(g_share)
        own, own_core, part = mlp_back(layer, g_share, slope[0], mlp_w, f32)
        g_far = after(g_far, part)
        far, far_core, there = mlp_back(layer, g_far, slope[1], mlp_w, bf16)
        arrived = swap_view(there)
        if layer == 0:
            arrived = after(arrived, got_attn1)
        back = (own, swap_core(own_core), far, swap_core(far_core))
        sums = mlp_sums(width, kept, after(back, *due))
        return sums, (part, after(arrived, sums))

    first_in = stream
    weights = (own_w[:1], far_w, w_out[:1], far_o)
    kept0, lse0, part, part_core = attend(place, view_counts, (a_share, swap_core(a_share)), weights)
    first_mid, b_share = join_norm(first_in, (part, swap_core(part_core)), gain_mlp[0])
    mlp0, slope0, terms = feed_forward(0, b_share)

    second_in, a_share = join_norm(first_mid, terms, gain_attn[1])
    a_far = swap_view(a_share)
    shares = (a_share, swap_core(a_share), a_far, swap_core(a_far))
    own1, far1, lse1, lse1_far, part, part_core, there, there_core = cross(
        place, view_counts, shares, own_w, w_out
    )
    arrived = swap_view((there + swap_core(there_core)).astype(bf16))
    second_mid, b_share = join_norm(second_in, (part, swap_core(part_core), arrived), gain_mlp[1])
    mlp1, slope1, terms = feed_forward(1, b_share)
    layer_output = (second_mid + terms[0] + terms[1].astype(f32)).astype(bf16)

    def along_z(values):
        groups = [list(range(s, peers, 2)) for s in range(2)]
        return lax.psum_scatter(
            values, "dp", scatter_dimension=0, tiled=True, axis_index_groups=groups
        )

    def between_sides(values):
        send = lax.dynamic_slice_in_dim(values, (1 - side[0]) * block, block, 0)
        keep = lax.dynamic_slice_in_dim(values, side[0] * block, block, 0)
        return keep.astype(f32) + swap_side(send).astype(f32)

    gain_parts = [None] * 4
    mlp_sum1, terms = feed_forward_back(1, cotangent, mlp1, slope1)
    sum_mlp1 = along_z(mlp_sum1)
    gain_parts[3], gradient, g_share = norm_back(second_mid, gain_mlp[1], cotangent, terms)

    g_far = swap_view(g_share)
    own_back = cross_back(
        1, place, view_counts, (g_share, swap_core(g_share)), own1, far1, lse1, w_out
    )
    g_far = after(g_far, own_back)
    far_back = cross_back(
        0, place, view_counts, (g_far, swap_core(g_far)), far1, own1, lse1_far, w_out
    )
    part, part_core, there, there_core = cross_rows(rows, width, own_back, far_back, own_w)
    arrived = swap_view((there + swap_core(there_core)).astype(bf16))
    attn_sum1 = cross_sums(width, mine, own1, far1, own_back, far_back)
    terms = (part, swap_core(part_core), after(arrived, attn_sum1))
    attn_cut = cut_outside(side, peers, attn_sum1)
    got_attn1 = swap_side(attn_cut[0])
    gain_parts[1], gradient, g_share = norm_back(second_in, gain_attn[1], gradient, terms)

    mlp_sum0, terms = feed_forward_back(0, g_share, mlp0, slope0)
    sum_mlp0 = along_z(after(mlp_sum0, sum_mlp1))
    gain_parts[2], gradient, g_share = norm_back(first_mid, gain_mlp[0], gradient, terms)

    back, part, part_core = attend_back(
        place, view_counts, (g_share, swap_core(g_share)), kept0, lse0, weights
    )
    back, layer_output = lax.optimization_barrier((back, layer_output))
    near, far, send, keep = attend_sums(side, peers, width, kept0, back)
    gain_parts[0], gradient, _ = norm_back(
        first_in, gain_attn[0], gradient, (part, swap_core(part_core))
    )

    (outgoing,) = run(
        give_body,
        [((peers, capacity + 8, width), bf16)],
        (slot, weight_row, gradient, *gain_parts),
        us=1.5,
    )
    returned = lax.all_to_all(outgoing, "dp", split_axis=0, concat_axis=0, tiled=True)

    got_far, got_send, _ = lax.optimization_barrier((swap_view(far), swap_side(send), outgoing))
    send_qk, keep_qk = cut_outside(side, peers, near + got_far.astype(f32))
    keep_vo = keep + got_send.astype(f32)
    n = near.shape[1]
    sum_qk = (keep_qk + swap_side(send_qk).astype(f32)).astype(bf16)
    sum_vo = (keep_vo[:, :, :n] + swap_view(keep_vo[:, :, n:].astype(bf16)).astype(f32)).astype(bf16)
    first_sum = (attn_cut[1].astype(f32) + got_attn1.astype(f32)).astype(bf16)
    joined = jnp.concatenate([sum_qk, sum_vo, first_sum], axis=2)
    joined = joined.reshape(peers // 2 * block, 8 * mine)
    joined, sum_mlp0, returned = lax.optimization_barrier((joined, sum_mlp0, returned))
    attn_sum = along_z(joined)
    mlp_all = jnp.stack([between_sides(sum_mlp0), between_sides(sum_mlp1)])
    gain_sum, part, part_core, there, there_core = run(
        spread_body,
        [((4, width), f32)] + [((rows, width), f32)] * 4,
        (place, asked, returned),
        us=1.5,
        scalars=(0,),
        scratch=[pltpu.VMEM((slots, width), bf16)],
    )
    gain_sum = gain_sum + swap_core(gain_sum)
    gain_sum = gain_sum + swap_view(gain_sum)
    gain_sum = lax.dynamic_slice_in_dim(gain_sum, lax.axis_index("dp") * block, block, 1)
    arrived = swap_view((there + swap_core(there_core)).astype(bf16))
    grad_tokens = weight_own * gradient + part + swap_core(part_core) + arrived.astype(f32)

    grad_qkv, grad_out = run(
        finish_body, [((2, 3, block, mine), f32), ((2, mine, block), f32)], (attn_sum,)
    )
    hidden = mlp_all.shape[-1] // 2
    return (
        layer_output,
        grad_tokens,
        grad_qkv.transpose(0, 2, 1, 3),
        grad_out,
        mlp_all[:, :, :hidden],
        mlp_all[:, :, hidden:].transpose(0, 2, 1),
        gain_sum[:2],
        gain_sum[2:],
    )


def solution(mesh):
    placed = (
        P("dp", None),
        P(("dp", "mp"), None),
        P(("dp", "mp")),
        P(("dp", "mp"), None),
        P(("dp", "mp")),
        P("dp", None),
        P(None, None, None, "mp"),
        P(None, "mp", None),
        P(None, None, "mp"),
        P(None, "mp", None),
        P(),
        P(),
    )
    return jax.shard_map(
        on_device,
        mesh=mesh,
        in_specs=placed,
        out_specs=(
            P(("dp", "mp"), None),
            P(("dp", "mp"), None),
            P(None, "dp", None, "mp"),
            P(None, "mp", "dp"),
            P(None, "dp", "mp"),
            P(None, "mp", "dp"),
            P(None, "dp"),
            P(None, "dp"),
        ),
        check_vma=False,
    )
```

```python
import functools

import jax
import jax.numpy as jnp
from jax import lax
from jax.experimental import pallas as pl
from jax.experimental.pallas import tpu as pltpu
from jax.sharding import PartitionSpec as P

HD = 64
SCALE = HD ** (-0.5)
epsilon = 1e-06
masked_score = -1000000000.0
bf16 = jnp.bfloat16
f32 = jnp.float32
i32 = jnp.int32

TAIL_P = 0.38
TAIL = (
    0.2144098248509563,
    0.21394460416600933,
    0.20368405029440034,
    0.13968567743708352,
    0.2272053511927878,
    -0.15681775904774625,
    0.3593185352386043,
    -0.25984971762641107,
    0.058419421394547984,
)


def dot(left, right):
    return jnp.dot(left, right, preferred_element_type=f32)


def dot_rt(left, right):
    return lax.dot_general(left, right, (((1,), (1,)), ((), ())), preferred_element_type=f32)


def dot_lt(left, right):
    return lax.dot_general(left, right, (((0,), (0,)), ((), ())), preferred_element_type=f32)


def swap_core(values):
    return lax.ppermute(values, "mp", [(i, i ^ 1) for i in range(4)])


def swap_view(values):
    return lax.ppermute(values, "mp", [(i, i ^ 2) for i in range(4)])


def swap_side(values):
    return lax.ppermute(values, "dp", [(i, i ^ 1) for i in range(lax.axis_size("dp"))])


def after(values, *others):
    return lax.optimization_barrier((values, *others))[0]


def run(body, outs, args, us=1.0, scalars=(), scratch=(), hidden=False, left=()):
    return pl.pallas_call(
        body,
        out_shape=[jax.ShapeDtypeStruct(s, d) for s, d in outs],
        in_specs=[
            pl.BlockSpec(
                memory_space=pltpu.SMEM if i in scalars else pl.ANY if i in left else pltpu.VMEM
            )
            for i in range(len(args))
        ],
        out_specs=[pl.BlockSpec(memory_space=pltpu.VMEM) for _ in outs],
        scratch_shapes=list(scratch),
        compiler_params=pltpu.CompilerParams(vmem_limit_bytes=VMEM_LIMIT),
        cost_estimate=pl.CostEstimate(
            flops=int(us * PEAK * (3 if hidden else 1)), bytes_accessed=0, transcendentals=0
        ),
    )(*args)


VMEM_LIMIT = 16 * 1024 * 1024
PEAK = 1.15e9


def norm_parts(values):
    centred = values - jnp.mean(values, axis=-1, keepdims=True)
    rstd = lax.rsqrt(jnp.mean(centred * centred, axis=-1, keepdims=True) + epsilon)
    return centred * rstd, rstd


def join_body(count, *refs):
    base, terms, gain = refs[0], refs[1 : 1 + count], refs[1 + count]
    total = base[...]
    for term in terms:
        total = total + term[...].astype(f32)
    refs[2 + count][...] = total
    refs[3 + count][...] = (norm_parts(total)[0] * gain[...]).astype(bf16)


def join_norm(base, terms, gain):
    outs = [(base.shape, f32), (base.shape, bf16)]
    body = functools.partial(join_body, len(terms))
    return run(body, outs, (base, *terms, gain[None]), us=1.1)


def norm_back_body(count, *refs):
    values, gain, gradient = refs[:3]
    total = refs[3][...].astype(f32)
    for term in refs[4 : 3 + count]:
        total = total + term[...].astype(f32)
    n, rstd = norm_parts(values[...])
    refs[3 + count][...] = jnp.sum(total * n, axis=0, keepdims=True)
    dn = total * gain[...]
    dx = rstd * (
        dn - jnp.mean(dn, axis=-1, keepdims=True) - n * jnp.mean(dn * n, axis=-1, keepdims=True)
    )
    new = gradient[...].astype(f32) + dx
    refs[4 + count][...] = new
    refs[5 + count][...] = new.astype(bf16)


def norm_back(values, gain, gradient, terms):
    outs = [((1, values.shape[1]), f32), (values.shape, f32), (values.shape, bf16)]
    body = functools.partial(norm_back_body, len(terms))
    return run(body, outs, (values, gain[None], gradient, *terms), us=1.5)


def finish_body(sums, qkv, out):
    m = out.shape[1]
    for layer in range(2):
        at = 4 * m * layer
        for i in range(3):
            qkv[layer, i] = sums[:, at + i * m : at + (i + 1) * m].astype(f32)
        out[layer] = sums[:, at + 3 * m : at + 4 * m].astype(f32).T


def ask_body(capacity, target, partner, slot_ref, ask_ref):
    peers = ask_ref.shape[0]
    rows = target.shape[1]
    chosen = lax.broadcasted_iota(i32, (peers, rows), 0) == target[...]
    earlier = lax.broadcasted_iota(i32, (rows, rows), 0) < lax.broadcasted_iota(
        i32, (rows, rows), 1
    )
    before = dot(jnp.where(chosen, 1.0, 0.0).astype(bf16), jnp.where(earlier, 1.0, 0.0).astype(bf16))
    rank = jnp.sum(jnp.where(chosen, before, 0.0), axis=0, keepdims=True).astype(i32)
    slot_ref[...] = target[...] * capacity + rank
    placed = lax.broadcasted_iota(i32, (capacity, rows), 0) == rank
    placed = jnp.where(placed, 1.0, 0.0).astype(bf16)
    high = partner[...] // 32
    low = partner[...] - high * 32
    part = lambda v: dot_rt(jnp.where(chosen, v.astype(f32), 0.0).astype(bf16), placed)
    ask_ref[...] = (part(high) * 32.0 + part(low)).astype(i32)


def one_hot(index, count):
    hit = lax.broadcasted_iota(i32, (count, index.shape[1]), 0) == index[...]
    return jnp.where(hit, 1.0, 0.0).astype(bf16)


def find_body(asked, tokens, found):
    found[...] = dot_lt(one_hot(asked, tokens.shape[0]), tokens[...]).astype(bf16)


def column(row):
    return jnp.broadcast_to(row[...], (8, row.shape[1])).T[:, :1]


def mix_body(place, slot, replies, tokens, weight, gain, stream, normed, own, sem):
    rows = own.shape[0]
    start = pl.multiple_of(place[0] * rows, rows)
    copy = pltpu.make_async_copy(tokens.at[pl.ds(start, rows), :], own, sem)
    copy.start()
    partner = dot_lt(one_hot(slot, replies.shape[0]), replies[...])
    mine = column(weight)
    copy.wait()
    total = mine * own[...].astype(f32) + (1.0 - mine) * partner
    stream[...] = total
    normed[...] = (norm_parts(total)[0] * gain[...]).astype(bf16)


def give_body(slot, weight, gradient, g0, g1, g2, g3, outgoing):
    peers, count, _ = outgoing.shape
    capacity = count - 8
    rows = ((1.0 - column(weight)) * gradient[...]).astype(bf16)
    placed = dot(one_hot(slot, peers * capacity), rows).astype(bf16)
    gains = jnp.concatenate([g0[...], g1[...], g2[...], g3[...]], axis=0)
    high = gains.astype(bf16)
    extra = jnp.concatenate([high.astype(f32), gains - high.astype(f32)], axis=0).astype(bf16)
    for p in range(peers):
        outgoing[p, :capacity, :] = placed[p * capacity : (p + 1) * capacity, :]
        outgoing[p, capacity:, :] = extra


def spread_body(place, asked, returned, gains, *refs):
    near, core, far, far_core, flat = refs
    peers, count, _ = returned.shape
    capacity = count - 8
    rows = near.shape[0]
    total = jnp.zeros((8, near.shape[1]), f32)
    for p in range(peers):
        flat[p * capacity : (p + 1) * capacity, :] = returned[p, :capacity, :]
        total = total + returned[p, capacity:, :].astype(f32)
    gains[...] = total[:4] + total[4:]
    for i, ref in enumerate((near, core, far, far_core)):
        owner = jnp.bitwise_xor(place[0], i)
        ref[...] = dot(one_hot(asked[...] - owner * rows, rows), flat[...])


def gelu_parts(u):
    t = 1.0 / (1.0 + (TAIL_P * 0.5**0.5) * jnp.abs(u))
    poly = TAIL[-1]
    for c in TAIL[-2::-1]:
        poly = poly * t + c
    bell = jnp.exp(-0.5 * u * u)
    tail = 0.5 * poly * t * bell
    phi = jnp.where(u < 0.0, tail, 1.0 - tail)
    return u * phi, phi + u * bell * 0.3989422804014327


def fetch(layer, sources, places, sems):
    copies = [
        pltpu.make_async_copy(source.at[layer], place, sems.at[i])
        for i, (source, place) in enumerate(zip(sources, places))
    ]
    for copy in copies:
        copy.start()
    return copies


def mlp_body(layer, b, up0, up1, down0, down1, mine, theirs, slope, part, up2, down2, sems):
    width = b.shape[1]
    hidden = up0.shape[2]
    rows = b[...]
    copies = fetch(layer, (up1, down1), (up2, down2), sems)
    total = 0.0
    sides = ((mine, up0.at[layer], down0.at[layer]), (theirs, up2, down2))
    for i, (saved, up, down) in enumerate(sides):
        saved[:, :width] = rows
        if i == 1:
            for copy in copies:
                copy.wait()
        for j in range(0, hidden, 256):
            z, dz = gelu_parts(dot(rows, up[:, j : j + 256]))
            saved[:, width + j : width + j + 256] = z.astype(bf16)
            slope[:, i * hidden + j : i * hidden + j + 256] = dz
        total = total + dot(saved[:, width:], down[...])
    part[...] = total.astype(part.dtype)


def fetched(weights):
    shapes = [pltpu.VMEM(w.shape[1:], w.dtype) for w in (weights[1], weights[3])]
    return [*shapes, pltpu.SemaphoreType.DMA((2,))]


def mlp(layer, b, weights, dtype):
    rows, width = b.shape
    hidden = weights[0].shape[2]
    outs = [((rows, width + hidden), bf16)] * 2
    outs += [((rows, 2 * hidden), f32), ((rows, width), dtype)]
    body = functools.partial(mlp_body, layer)
    return run(body, outs, (b, *weights), us=3.5, scratch=fetched(weights), left=(2, 4))


def mlp_back_body(
    layer, g, slope, up0, up1, down0, down1, mine, theirs, part, up2, down2, sems
):
    width = g.shape[1]
    hidden = up0.shape[2]
    rows = g[...]
    copies = fetch(layer, (up1, down1), (up2, down2), sems)
    total = 0.0
    sides = ((mine, up0.at[layer], down0.at[layer]), (theirs, up2, down2))
    for i, (saved, up, down) in enumerate(sides):
        saved[:, :width] = rows
        if i == 1:
            for copy in copies:
                copy.wait()
        for j in range(0, hidden, 256):
            at = i * hidden + j
            dz = dot_rt(rows, down[j : j + 256, :])
            saved[:, width + j : width + j + 256] = (dz * slope[:, at : at + 256]).astype(bf16)
        total = total + dot_rt(saved[:, width:], up[...])
    part[...] = total.astype(part.dtype)


def mlp_back(layer, g, slope, weights, dtype):
    rows, width = g.shape
    hidden = weights[0].shape[2]
    outs = [((rows, width + hidden), bf16)] * 2 + [((rows, width), dtype)]
    body = functools.partial(mlp_back_body, layer)
    return run(body, outs, (g, slope, *weights), us=2.5, scratch=fetched(weights), left=(3, 5))


def mlp_sums_body(*refs):
    ahead, back, sums = refs[:4], refs[4:8], refs[8]
    width = sums.shape[0]
    hidden = sums.shape[1] // 2
    for i, (left, right) in enumerate(((ahead, back), (back, ahead))):
        left = jnp.concatenate([v[:, :width] for v in left], axis=0)
        right = jnp.concatenate([v[:, width:] for v in right], axis=0)
        sums[:, i * hidden : (i + 1) * hidden] = dot_lt(left, right).astype(bf16)


def mlp_sums(width, ahead, back):
    outs = [((width, 2 * (ahead[0].shape[1] - width)), bf16)]
    return run(mlp_sums_body, outs, (*ahead, *back), us=3.5, hidden=True)[0]


def cut_rows(side, values, send, keep, column):
    count, block, _ = send.shape
    n = values.shape[1]
    for z in range(count):
        theirs = pl.multiple_of((2 * z + 1 - side[0]) * block, 8)
        mine = pl.multiple_of((2 * z + side[0]) * block, 8)
        send[z, :, column : column + n] = values[pl.ds(theirs, block), :].astype(bf16)
        keep[z, :, column : column + n] = values[pl.ds(mine, block), :]


def cut_outside(side, peers, grads):
    parts = grads.reshape(peers // 2, 2, -1, grads.shape[1])
    send = lax.dynamic_index_in_dim(parts, 1 - side[0], 1, False)
    return send.astype(bf16), lax.dynamic_index_in_dim(parts, side[0], 1, False)


def groups_of(n):
    return [(j, min(128, n - j)) for j in range(0, n, 128)]


def places(width, n):
    stride = -(-n // 128) * 128
    return [width + i * stride for i in range(5)]


def view_bias(rows, place, counts, other):
    half = lax.rem(place[0], 2)
    count = counts[0, jnp.bitwise_xor(lax.div(place[0], 2), other)]
    index = lax.broadcasted_iota(i32, (2 * rows, 1), 0)
    position = jnp.where(index < rows, index + half * rows, index - half * rows)
    return jnp.where(position < count, 0.0, masked_score).astype(f32)


def masked(values, head):
    if values.shape[1] == HD:
        return values
    keep = lax.broadcasted_iota(i32, values.shape, 1) // HD == head
    return jnp.where(keep, values, jnp.zeros_like(values))


def attend_core(from_q, from_k, lse, bias, width, n):
    q0, k0, v0, o0, _ = places(width, n)
    lse[...] = jnp.zeros(lse.shape, f32)
    for j, w in groups_of(n):
        q = from_q[:, q0 + j : q0 + j + w] * jnp.asarray(SCALE, bf16)
        k = from_k[:, k0 + j : k0 + j + w]
        v = from_k[:, v0 + j : v0 + j + w]
        out = jnp.zeros((w, q.shape[0]), f32)
        for head in range(w // HD):
            s = dot_rt(k, masked(q, head)) + bias
            top = jnp.max(s, axis=0, keepdims=True)
            e = jnp.exp(s - top)
            total = jnp.sum(e, axis=0, keepdims=True)
            weights = (e * (1.0 / total)).astype(bf16)
            at = j // HD + head
            lse[at : at + 1, :] = top + jnp.log(total)
            out = out + dot_lt(masked(v, head), weights)
        from_q[:, o0 + j : o0 + j + w] = out.T.astype(bf16)


def attend_back_core(from_q, from_k, do, lse, bias, back, width, n):
    q0, k0, v0, _, _ = places(width, n)
    for j, w in groups_of(n):
        q = from_q[:, q0 + j : q0 + j + w] * jnp.asarray(SCALE, bf16)
        k = from_k[:, k0 + j : k0 + j + w]
        v = from_k[:, v0 + j : v0 + j + w]
        d = do[:, j : j + w]
        dv = jnp.zeros(q.shape, f32)
        dk = jnp.zeros(q.shape, f32)
        dq = jnp.zeros((w, q.shape[0]), f32)
        for head in range(w // HD):
            qm, dm, km = masked(q, head), masked(d, head), masked(k, head)
            at = j // HD + head
            p = jnp.exp(dot_rt(k, qm) + bias - lse[at : at + 1, :])
            dp = dot_rt(v, dm)
            centre = jnp.sum(p * dp, axis=0, keepdims=True)
            ds = (p * (dp - centre)).astype(bf16)
            dv = dv + dot(p.astype(bf16), dm)
            dk = dk + dot(ds, qm)
            dq = dq + dot_lt(km, ds)
        back[:, q0 + j : q0 + j + w] = (dq.T * SCALE).astype(bf16)
        back[:, k0 + j : k0 + j + w] = dk.astype(bf16)
        back[:, v0 + j : v0 + j + w] = dv.astype(bf16)


def join_weights(own, far, own_o, far_o, w, wo):
    m = own_o.shape[1]
    for i in range(3):
        w[2 * i * m : (2 * i + 1) * m, :] = own[0, i]
        w[(2 * i + 1) * m : (2 * i + 2) * m, :] = far[0, i]
    wo[:m, :] = own_o[0]
    wo[m:, :] = far_o[0]


def attend_body(place, counts, a0, a1, own, far, own_o, far_o, saved, lse, p0, p1, w, wo):
    join_weights(own, far, own_o, far_o, w, wo)
    rows, width = p0.shape
    n = wo.shape[0]
    q0, _, _, o0, _ = places(width, n)
    a = jnp.concatenate([a0[...], a1[...]], axis=0)
    saved[:, :width] = a
    saved[:, q0:o0] = dot_rt(a, w[...]).astype(bf16)
    attend_core(saved, saved, lse, view_bias(rows, place, counts, 0), width, n)
    p0[...] = dot(saved[:rows, o0:], wo[...])
    p1[...] = dot(saved[rows:, o0:], wo[...])


def attend(place, counts, shares, weights):
    rows, width = shares[0].shape
    n = 2 * weights[2].shape[1]
    outs = [((2 * rows, width + 4 * n), bf16), ((8, 2 * rows), f32)]
    outs += [((rows, width), f32)] * 2
    scratch = [pltpu.VMEM((3 * n, width), bf16), pltpu.VMEM((n, width), bf16)]
    return run(
        attend_body,
        outs,
        (place, counts, *shares, *weights),
        us=6.5,
        scalars=(0, 1),
        scratch=scratch,
    )


def attend_back_body(
    place, counts, g0, g1, saved, lse, own, far, own_o, far_o, back, p0, p1, do, w, wo
):
    join_weights(own, far, own_o, far_o, w, wo)
    rows, width = g0.shape
    n = wo.shape[0]
    g = jnp.concatenate([g0[...], g1[...]], axis=0)
    back[:, :width] = g
    do[...] = dot_rt(g, wo[...]).astype(bf16)
    bias = view_bias(rows, place, counts, 0)
    attend_back_core(saved, saved, do, lse, bias, back, width, n)
    p0[...] = dot(back[:rows, width:], w[...])
    p1[...] = dot(back[rows:, width:], w[...])


def attend_back(place, counts, g, saved, lse, weights):
    rows, width = g[0].shape
    n = 2 * weights[2].shape[1]
    return run(
        attend_back_body,
        [((2 * rows, width + 3 * n), bf16)] + [((rows, width), f32)] * 2,
        (place, counts, *g, saved, lse, *weights),
        us=8.0,
        scalars=(0, 1),
        scratch=[
            pltpu.VMEM((2 * rows, n), bf16),
            pltpu.VMEM((3 * n, width), bf16),
            pltpu.VMEM((n, width), bf16),
        ],
    )


def attend_sums_body(cut, side, saved, back, near, far, *refs):
    total = refs[-1]
    width, n = near.shape
    m = n // 2
    q0, k0, v0, o0, _ = places(width, n)
    a = saved[:, :width]
    for i in range(2):
        part = dot_lt(a, back[:, q0 + i * n : q0 + (i + 1) * n])
        near[:, i * m : (i + 1) * m] = part[:, :m]
        far[:, i * m : (i + 1) * m] = part[:, m:].astype(bf16)
    for i in range(2):
        if i == 0:
            part = dot_lt(a, back[:, v0 : v0 + n])
        else:
            part = dot_lt(back[:, :width], saved[:, o0 : o0 + n])
        total[:, i * m : (i + 1) * m] = part[:, :m]
        total[:, n + i * m : n + (i + 1) * m] = part[:, m:]
    if cut:
        cut_rows(side, total, refs[0], refs[1], 0)


def attend_sums(side, peers, width, saved, back):
    n = (saved.shape[1] - width) // 4
    block = width // peers
    cut = block % 16 == 0
    outs = [((width, n), f32), ((width, n), bf16)]
    scratch = []
    if cut:
        outs += [((peers // 2, block, 2 * n), bf16), ((peers // 2, block, 2 * n), f32)]
        scratch = [pltpu.VMEM((width, 2 * n), f32)]
    else:
        outs += [((width, 2 * n), f32)]
    out = run(
        functools.partial(attend_sums_body, cut),
        outs,
        (side, saved, back),
        us=3.0,
        scalars=(0,),
        scratch=scratch,
    )
    return out if cut else (*out[:2], *cut_outside(side, peers, out[2]))


def cross_body(
    place, counts, a0, a1, a2, a3, w, wo, own, far, lse, lse_far, p0, p1, p2, p3
):
    rows, width = p0.shape
    n = wo.shape[1]
    q0, k0, v0, o0, _ = places(width, n)
    for saved, halves in ((own, (a0, a1)), (far, (a2, a3))):
        a = jnp.concatenate([halves[0][...], halves[1][...]], axis=0)
        saved[:, :width] = a
        for i, at in enumerate((q0, k0, v0)):
            saved[:, at : at + n] = dot_rt(a, w[1, i]).astype(bf16)
    attend_core(far, own, lse_far, view_bias(rows, place, counts, 0), width, n)
    p2[...] = dot(far[:rows, o0 : o0 + n], wo[1])
    p3[...] = dot(far[rows:, o0 : o0 + n], wo[1])
    attend_core(own, far, lse, view_bias(rows, place, counts, 1), width, n)
    p0[...] = dot(own[:rows, o0 : o0 + n], wo[1])
    p1[...] = dot(own[rows:, o0 : o0 + n], wo[1])


def cross(place, counts, shares, w, wo):
    rows, width = shares[0].shape
    wide = places(width, wo.shape[1])[4]
    outs = [((2 * rows, wide), bf16)] * 2 + [((8, 2 * rows), f32)] * 2
    outs += [((rows, width), f32)] * 4
    args = (place, counts, *shares, w, wo)
    return run(cross_body, outs, args, us=6.5, scalars=(0, 1))


def cross_back_body(other, place, counts, g0, g1, from_q, from_k, lse, wo, back, do):
    rows, width = g0.shape
    n = wo.shape[1]
    g = jnp.concatenate([g0[...], g1[...]], axis=0)
    back[:, :width] = g
    do[...] = dot_rt(g, wo[1]).astype(bf16)
    bias = view_bias(rows, place, counts, other)
    attend_back_core(from_q, from_k, do, lse, bias, back, width, n)


def cross_back(other, place, counts, g, from_q, from_k, lse, wo):
    rows, width = g[0].shape
    n = wo.shape[1]
    return run(
        functools.partial(cross_back_body, other),
        [((2 * rows, places(width, n)[3]), bf16)],
        (place, counts, *g, from_q, from_k, lse, wo),
        us=4.0,
        scalars=(0, 1),
        scratch=[pltpu.VMEM((2 * rows, n), bf16)],
    )[0]


def cross_rows_body(own, far, w, p0, p1, p2, p3):
    rows, width = p0.shape
    n = w.shape[2]
    q0, k0, v0, _, _ = places(width, n)
    for queries, keys, parts in ((far, own, (p2, p3)), (own, far, (p0, p1))):
        for i, part in enumerate(parts):
            at = slice(i * rows, (i + 1) * rows)
            part[...] = (
                dot(queries[at, q0 : q0 + n], w[1, 0])
                + dot(keys[at, k0 : k0 + n], w[1, 1])
                + dot(keys[at, v0 : v0 + n], w[1, 2])
            )


def cross_rows(rows, width, own, far, w):
    return run(cross_rows_body, [((rows, width), f32)] * 4, (own, far, w), us=2.0)


def cross_sums_body(own, far, own_back, far_back, sums):
    width = sums.shape[0]
    n = sums.shape[1] // 4
    q0, k0, v0, o0, _ = places(width, n)
    rows = lambda first, second, at, size: jnp.concatenate(
        [first[:, at : at + size], second[:, at : at + size]], axis=0
    )
    queries = rows(own, far, 0, width)
    keys = rows(far, own, 0, width)
    parts = [
        (queries, rows(own_back, far_back, q0, n)),
        (keys, rows(own_back, far_back, k0, n)),
        (keys, rows(own_back, far_back, v0, n)),
        (rows(own_back, far_back, 0, width), rows(own, far, o0, n)),
    ]
    for i, (left, right) in enumerate(parts):
        sums[:, i * n : (i + 1) * n] = dot_lt(left, right).astype(bf16)


def cross_sums(width, n, own, far, own_back, far_back):
    return run(
        cross_sums_body, [((width, 4 * n), bf16)], (own, far, own_back, far_back), us=3.0
    )[0]


def on_device(
    tokens,
    cotangent,
    mix_coef,
    partner_dev,
    partner_row,
    view_counts,
    w_qkv,
    w_out,
    w_up,
    w_down,
    gain_attn,
    gain_mlp,
):
    peers = lax.axis_size("dp")
    rows = mix_coef.shape[0]
    width = tokens.shape[1]
    mine = w_qkv.shape[-1]
    block = width // peers
    capacity = max(2, 2 * rows // peers)
    slots = peers * capacity
    place = lax.axis_index("mp").astype(i32)[None]
    side = (lax.axis_index("dp") % 2).astype(i32)[None]
    weight_own = mix_coef[:, None]
    weight_row = mix_coef[None]

    slot, requests = run(
        functools.partial(ask_body, capacity),
        [((1, rows), i32), ((peers, capacity), i32)],
        (partner_dev.reshape(1, rows), partner_row.reshape(1, rows)),
    )

    own_w = w_qkv.transpose(0, 2, 3, 1)
    far_o = swap_view(w_out[:1])
    far_w = swap_view(own_w[:1])
    asked = lax.all_to_all(requests, "dp", split_axis=0, concat_axis=0, tiled=True)
    asked = after(asked, far_o).reshape(1, slots)
    (found,) = run(find_body, [((slots, width), bf16)], (asked, tokens), us=2.0)
    replies = lax.all_to_all(
        found.reshape(peers, capacity, width), "dp", split_axis=0, concat_axis=0, tiled=True
    )
    replies, far_w = lax.optimization_barrier((replies, far_w))
    stream, a_share = run(
        mix_body,
        [((rows, width), f32), ((rows, width), bf16)],
        (place, slot, replies.reshape(slots, width), tokens, weight_row, gain_attn[:1]),
        us=1.5,
        scalars=(0,),
        left=(3,),
        scratch=[pltpu.VMEM((rows, width), tokens.dtype), pltpu.SemaphoreType.DMA],
    )
    mlp_w = (w_up, swap_core(w_up), w_down, swap_core(w_down))

    def feed_forward(layer, b_share):
        b_far = swap_view(b_share)
        own, own_core, slope_own, part = mlp(layer, b_share, mlp_w, f32)
        far, far_core, slope_far, there = mlp(layer, after(b_far, part), mlp_w, bf16)
        kept = (own, swap_core(own_core), far, swap_core(far_core))
        return kept, (slope_own, slope_far), (part, swap_view(there))

    def feed_forward_back(layer, g_share, kept, slope, due=()):
        g_far = swap_view(g_share)
        own, own_core, part = mlp_back(layer, g_share, slope[0], mlp_w, f32)
        g_far = after(g_far, part)
        far, far_core, there = mlp_back(layer, g_far, slope[1], mlp_w, bf16)
        arrived = swap_view(there)
        if layer == 0:
            arrived = after(arrived, got_attn1)
        back = (own, swap_core(own_core), far, swap_core(far_core))
        sums = mlp_sums(width, kept, after(back, *due))
        return sums, (part, after(arrived, sums))

    first_in = stream
    weights = (own_w[:1], far_w, w_out[:1], far_o)
    kept0, lse0, part, part_core = attend(place, view_counts, (a_share, swap_core(a_share)), weights)
    first_mid, b_share = join_norm(first_in, (part, swap_core(part_core)), gain_mlp[0])
    mlp0, slope0, terms = feed_forward(0, b_share)

    second_in, a_share = join_norm(first_mid, terms, gain_attn[1])
    a_far = swap_view(a_share)
    shares = (a_share, swap_core(a_share), a_far, swap_core(a_far))
    own1, far1, lse1, lse1_far, part, part_core, there, there_core = cross(
        place, view_counts, shares, own_w, w_out
    )
    arrived = swap_view((there + swap_core(there_core)).astype(bf16))
    second_mid, b_share = join_norm(second_in, (part, swap_core(part_core), arrived), gain_mlp[1])
    mlp1, slope1, terms = feed_forward(1, b_share)
    layer_output = (second_mid + terms[0] + terms[1].astype(f32)).astype(bf16)

    def along_z(values):
        groups = [list(range(s, peers, 2)) for s in range(2)]
        return lax.psum_scatter(
            values, "dp", scatter_dimension=0, tiled=True, axis_index_groups=groups
        )

    def between_sides(values):
        send = lax.dynamic_slice_in_dim(values, (1 - side[0]) * block, block, 0)
        keep = lax.dynamic_slice_in_dim(values, side[0] * block, block, 0)
        return keep.astype(f32) + swap_side(send).astype(f32)

    gain_parts = [None] * 4
    mlp_sum1, terms = feed_forward_back(1, cotangent, mlp1, slope1)
    sum_mlp1 = along_z(mlp_sum1)
    gain_parts[3], gradient, g_share = norm_back(second_mid, gain_mlp[1], cotangent, terms)

    g_far = swap_view(g_share)
    own_back = cross_back(
        1, place, view_counts, (g_share, swap_core(g_share)), own1, far1, lse1, w_out
    )
    g_far = after(g_far, own_back)
    far_back = cross_back(
        0, place, view_counts, (g_far, swap_core(g_far)), far1, own1, lse1_far, w_out
    )
    part, part_core, there, there_core = cross_rows(rows, width, own_back, far_back, own_w)
    arrived = swap_view((there + swap_core(there_core)).astype(bf16))
    attn_sum1 = cross_sums(width, mine, own1, far1, own_back, far_back)
    terms = (part, swap_core(part_core), after(arrived, attn_sum1))
    attn_cut = cut_outside(side, peers, attn_sum1)
    got_attn1 = swap_side(attn_cut[0])
    gain_parts[1], gradient, g_share = norm_back(second_in, gain_attn[1], gradient, terms)

    mlp_sum0, terms = feed_forward_back(0, g_share, mlp0, slope0)
    sum_mlp0 = along_z(after(mlp_sum0, sum_mlp1))
    gain_parts[2], gradient, g_share = norm_back(first_mid, gain_mlp[0], gradient, terms)

    back, part, part_core = attend_back(
        place, view_counts, (g_share, swap_core(g_share)), kept0, lse0, weights
    )
    back, layer_output = lax.optimization_barrier((back, layer_output))
    near, far, send, keep = attend_sums(side, peers, width, kept0, back)
    gain_parts[0], gradient, _ = norm_back(
        first_in, gain_attn[0], gradient, (part, swap_core(part_core))
    )

    (outgoing,) = run(
        give_body,
        [((peers, capacity + 8, width), bf16)],
        (slot, weight_row, gradient, *gain_parts),
        us=1.5,
    )
    returned = lax.all_to_all(outgoing, "dp", split_axis=0, concat_axis=0, tiled=True)

    got_far, got_send, _ = lax.optimization_barrier((swap_view(far), swap_side(send), outgoing))
    send_qk, keep_qk = cut_outside(side, peers, near + got_far.astype(f32))
    keep_vo = keep + got_send.astype(f32)
    n = near.shape[1]
    sum_qk = (keep_qk + swap_side(send_qk).astype(f32)).astype(bf16)
    sum_vo = (keep_vo[:, :, :n] + swap_view(keep_vo[:, :, n:].astype(bf16)).astype(f32)).astype(bf16)
    first_sum = (attn_cut[1].astype(f32) + got_attn1.astype(f32)).astype(bf16)
    joined = jnp.concatenate([sum_qk, sum_vo, first_sum], axis=2)
    joined = joined.reshape(peers // 2 * block, 8 * mine)
    joined = after(joined, sum_mlp0)
    attn_sum = along_z(joined)
    sum_mlp0, returned = lax.optimization_barrier((sum_mlp0, returned))
    mlp_all = jnp.stack([between_sides(sum_mlp0), between_sides(sum_mlp1)])
    gain_sum, part, part_core, there, there_core = run(
        spread_body,
        [((4, width), f32)] + [((rows, width), f32)] * 4,
        (place, asked, returned),
        us=1.5,
        scalars=(0,),
        scratch=[pltpu.VMEM((slots, width), bf16)],
    )
    gain_sum = gain_sum + swap_core(gain_sum)
    gain_sum = gain_sum + swap_view(gain_sum)
    gain_sum = lax.dynamic_slice_in_dim(gain_sum, lax.axis_index("dp") * block, block, 1)
    arrived = swap_view((there + swap_core(there_core)).astype(bf16))
    grad_tokens = weight_own * gradient + part + swap_core(part_core) + arrived.astype(f32)

    grad_qkv, grad_out = run(
        finish_body, [((2, 3, block, mine), f32), ((2, mine, block), f32)], (attn_sum,)
    )
    hidden = mlp_all.shape[-1] // 2
    return (
        layer_output,
        grad_tokens,
        grad_qkv.transpose(0, 2, 1, 3),
        grad_out,
        mlp_all[:, :, :hidden],
        mlp_all[:, :, hidden:].transpose(0, 2, 1),
        gain_sum[:2],
        gain_sum[2:],
    )


def solution(mesh):
    placed = (
        P("dp", None),
        P(("dp", "mp"), None),
        P(("dp", "mp")),
        P(("dp", "mp"), None),
        P(("dp", "mp")),
        P("dp", None),
        P(None, None, None, "mp"),
        P(None, "mp", None),
        P(None, None, "mp"),
        P(None, "mp", None),
        P(),
        P(),
    )
    return jax.shard_map(
        on_device,
        mesh=mesh,
        in_specs=placed,
        out_specs=(
            P(("dp", "mp"), None),
            P(("dp", "mp"), None),
            P(None, "dp", None, "mp"),
            P(None, "mp", "dp"),
            P(None, "dp", "mp"),
            P(None, "mp", "dp"),
            P(None, "dp"),
            P(None, "dp"),
        ),
        check_vma=False,
    )
```
